512 devices in a mesh: blk: 64 (over z, y_hi, core), dim: 8 (over y_lo, x).
Axes of the slice: x: 4, y: 4 (y_hi: 2, y_lo: 2; y = y_hi * 2 + y_lo), z: 16, core: 2. Of those that a mesh axis runs over, the one named last changes fastest.
Arguments:
- queries: bfloat16 [12288, 4096], P('blk', 'dim')
- passages: bfloat16 [12288, 4096], P('blk', 'dim')
- negatives: bfloat16 [24576, 4096], P('blk', 'dim')
- hard_index: int32 [12288, 7], P('blk'), may hold values from 0 to 24575, as said below
Outputs:
- grad_queries: float32 [12288, 4096], P('blk', 'dim')
- document_derivative: float32 [12288, 4096], P('blk', 'dim')
- grad_negatives: float32 [24576, 4096], P('blk', 'dim')
The draws below stay inside these ranges and needn't reach their ends.
Inputs may be any that keep to these rules, and one draw needn't show every extreme that they name: `hard_index`: pool rows are owned in blocks of 384: row r belongs to block r // 384. The 1344 entries of one block of queries name at most 42 rows of any one owning block, and exactly 42 rows of one owning block that is the same for every block of queries; entries may repeat.
All inputs are finite; a program needn't handle non-finite values.
Results may differ from the reference program's by a relative error of at most 0.012.
Values may be sent and summed in bfloat16 or wider, within the bound.
A program may use at most 128 MiB of HBM per device.

```python
import math
import jax
import jax.numpy as jnp
from jax import lax

D = 4096
Q_DEV = 192
WINDOW = 16
HARD = 7
NEG_DEV = 384
BATCH = 12288
NEGS = 24576
CAP = 42


positive_share = 0.21


hard_share = 0.14


near_share = 0.1


near_per_block = 4


start_picks = 12


def scaled_rows(key, rows, top_scale):
    first_key, second_key = jax.random.split(key)
    base = jax.random.normal(first_key, (rows, D), jnp.float32) * D ** (-0.5)
    spread = jax.random.uniform(second_key, (rows, 1), jnp.float32)
    return (base, jnp.exp(spread * math.log(top_scale)))


def passage_rows(key, top_scale):
    return scaled_rows(jax.random.fold_in(key, 21), BATCH, top_scale)


def pool_rows(key, top_scale):
    base, scales = scaled_rows(jax.random.fold_in(key, 22), NEGS, top_scale)
    return base


def hard_rows_of(key):
    key = jax.random.fold_in(key, 5)
    block_count = BATCH // Q_DEV
    wanted = HARD * Q_DEV
    hot_key, order_key, row_key = jax.random.split(key, 3)
    hottest = jax.random.randint(hot_key, (), 0, block_count, dtype=jnp.int32)

    def one_device(device_key):
        first_key, second_key = jax.random.split(device_key)
        others = jax.random.permutation(first_key, (block_count - 1) * CAP)[:wanted - CAP] // CAP
        others = (others + (others >= hottest).astype(jnp.int32)).astype(jnp.int32)
        owners = jnp.concatenate([jnp.full((CAP,), hottest, jnp.int32), others])
        return jax.random.permutation(second_key, owners)
    owners = jax.vmap(one_device)(jax.random.split(order_key, block_count))
    within = jax.random.randint(row_key, (block_count, wanted), 0, NEG_DEV, dtype=jnp.int32)
    return (owners * NEG_DEV + within).reshape(BATCH, HARD).astype(jnp.int32)


def shuffled_columns(order_key):
    return jax.random.permutation(order_key, Q_DEV).astype(jnp.int32)


def draw_hard_index(key, part):
    return hard_rows_of(key)


def draw_passages(key, part):
    base, scales = passage_rows(key, 1.0)
    return base.astype(jnp.bfloat16)


def draw_negatives(key, part):
    pool = pool_rows(key, 1.0)
    return pool.astype(jnp.bfloat16)


def draw_queries(key, part):
    base, scales = passage_rows(key, 1.0)
    pool = pool_rows(key, 1.0)
    passages = base
    hard_index = hard_rows_of(key)
    key = jax.random.fold_in(key, 11)
    noise_key, start_key, order_key, factor_key = jax.random.split(key, 4)
    position = jnp.arange(BATCH, dtype=jnp.int32)
    block_count = BATCH // Q_DEV
    reach = WINDOW - 1
    near_count = near_per_block * reach
    factors = 0.85 + 0.3 * jax.random.uniform(factor_key, (3, BATCH, 1), jnp.float32)
    positive_coef = positive_share * factors[0]
    hard_coef = hard_share * factors[1]
    near_coef = near_share * (0.9 + (factors[2] - 0.85) / 1.5)
    rest_coef = math.sqrt(1.0 - positive_share ** 2 - HARD * hard_share ** 2 - near_count * near_share ** 2)
    hard_total = jnp.zeros((BATCH, D), jnp.float32)
    for slot in range(HARD):
        hard_total = hard_total + pool[hard_index[:, slot]]
    starts = jnp.min(jax.random.randint(start_key, (BATCH, reach, start_picks), 0, Q_DEV, dtype=jnp.int32), axis=2)
    orders = jax.vmap(shuffled_columns)(jax.random.split(order_key, block_count)).reshape(-1)
    target = ((position[:, None] // Q_DEV + jnp.arange(1, WINDOW, dtype=jnp.int32)[None, :]) % block_count).astype(jnp.int32)
    within = ((starts[:, :, None] + jnp.arange(near_per_block, dtype=jnp.int32)[None, None, :]) % Q_DEV).astype(jnp.int32)
    near_rows = (target[:, :, None] * Q_DEV + orders[target[:, :, None] * Q_DEV + within]).reshape(BATCH, near_count).astype(jnp.int32)

    def add_near(slot, total):
        rows_now = lax.dynamic_index_in_dim(near_rows, slot, 1, keepdims=False)
        return total + passages[rows_now]
    near_total = lax.fori_loop(0, near_count, add_near, jnp.zeros((BATCH, D), jnp.float32))
    noise = jax.random.normal(noise_key, (BATCH, D), jnp.float32) * D ** (-0.5)
    length = jnp.sqrt(positive_coef ** 2 + HARD * hard_coef ** 2 + near_count * near_coef ** 2 + rest_coef ** 2)
    result = (positive_coef * passages + hard_coef * hard_total + near_coef * near_total + rest_coef * noise) / length
    return result.astype(jnp.bfloat16)


def setup_inputs(seed: int = 0) -> dict:
    seeds = jax.random.split(jax.random.key(seed), 5)
    return {
        "queries": draw_queries(jax.random.fold_in(seeds[4], 71), 0),
        "passages": draw_passages(jax.random.fold_in(seeds[4], 71), 0),
        "negatives": draw_negatives(jax.random.fold_in(seeds[4], 71), 0),
        "hard_index": draw_hard_index(jax.random.fold_in(seeds[4], 71), 0),
    }


logit_divisor = 0.02


def reference(queries, passages, negatives, hard_index):
    block_count = BATCH // Q_DEV
    offsets = jnp.arange(WINDOW * Q_DEV, dtype=jnp.int32)
    positive = (offsets[None, :] == jnp.arange(Q_DEV, dtype=jnp.int32)[:, None]).astype(jnp.float32)

    def one_block(carry, block_index):
        document_derivative_piece, grad_neg = carry
        start = (block_index * Q_DEV).astype(jnp.int32)
        question_matrix_slab = lax.dynamic_slice_in_dim(queries, start, Q_DEV, 0)
        adjacent_reach_vectors = ((start + offsets) % BATCH).astype(jnp.int32)
        adjacent_reach = passages[adjacent_reach_vectors]
        hard_ids = lax.dynamic_slice_in_dim(hard_index, start, Q_DEV, 0)
        mined_foil_vectors = negatives[hard_ids]
        cosine_logits = jnp.dot(question_matrix_slab, adjacent_reach.T, preferred_element_type=jnp.float32) / logit_divisor
        mined_foil_logits = jnp.einsum("eo,ezo->ez", question_matrix_slab.astype(jnp.float32), mined_foil_vectors.astype(jnp.float32)) / logit_divisor
        row_max = jnp.maximum(jnp.max(cosine_logits, axis=1), jnp.max(mined_foil_logits, axis=1))
        row_total = jnp.sum(jnp.exp(cosine_logits - row_max[:, None]), axis=1) + jnp.sum(jnp.exp(mined_foil_logits - row_max[:, None]), axis=1)
        log_total = row_max + jnp.log(row_total)
        normalized_probabilities = (jnp.exp(cosine_logits - log_total[:, None]) - positive).astype(jnp.bfloat16)
        mined_foil_probabilities = jnp.exp(mined_foil_logits - log_total[:, None]).astype(jnp.bfloat16)
        grad_query = (jnp.dot(normalized_probabilities, adjacent_reach, preferred_element_type=jnp.float32)
                      + jnp.einsum("em,emz->ez", mined_foil_probabilities.astype(jnp.float32), mined_foil_vectors.astype(jnp.float32))) / logit_divisor
        document_derivative_piece = document_derivative_piece.at[adjacent_reach_vectors].add(jnp.dot(normalized_probabilities.T, question_matrix_slab, preferred_element_type=jnp.float32) / logit_divisor)
        relayed_vectors = (mined_foil_probabilities.astype(jnp.float32)[:, :, None] * question_matrix_slab.astype(jnp.float32)[:, None, :] / logit_divisor).astype(jnp.bfloat16)
        grad_neg = grad_neg.at[hard_ids.reshape(-1)].add(relayed_vectors.reshape(-1, D).astype(jnp.float32))
        return (document_derivative_piece, grad_neg), grad_query

    start_carry = (jnp.zeros((BATCH, D), jnp.float32), jnp.zeros((NEGS, D), jnp.float32))
    (document_derivative, grad_negatives), grad_blocks = lax.scan(one_block, start_carry, jnp.arange(block_count, dtype=jnp.int32))
    return grad_blocks.reshape(BATCH, D), document_derivative, grad_negatives
```

```python
import functools

import jax
import jax.numpy as jnp
from jax import lax
from jax.experimental import pallas as pl
from jax.experimental.pallas import tpu as pltpu
from jax.sharding import PartitionSpec as P

WINDOW = 16
HARD = 7
PLANE = 4
REACH = WINDOW // PLANE
SUB = 2
LOW = -1e30

logit_divisor = 0.02
scale = 1.0 / logit_divisor

F32, BF16 = jnp.float32, jnp.bfloat16
MESH = pl.DeviceIdType.MESH


def dot(left, right, left_dim, right_dim):
    return lax.dot_general(
        left, right, (((left_dim,), (right_dim,)), ((), ())), preferred_element_type=F32
    )


def remote(src, dst, send_sem, recv_sem, device):
    return pltpu.make_async_remote_copy(
        src_ref=src,
        dst_ref=dst,
        send_sem=send_sem,
        recv_sem=recv_sem,
        device_id=device,
        device_id_type=MESH,
    )


def loop(low, high, body):
    def step(index, carry):
        body(index)
        return carry

    lax.fori_loop(low, high, step, 0)


def kernel(
    planes, dims,
    q_in, p_in, n_in, idx_in, gq_out, dp_out, dn_out,
    qbuf, idxb, pbuf, nbuf, qcat, st, rbuf, sc, hp, hrecv, wsend, wrecv, msg, arecv, hwb,
    wt, wht, cbuf, win, dnb, dpb, recva, recvb, senda, sendb, csend, crecv, ysend, yrecv,
    loc, us, ur, ds, dr, ps, pr, ns, nr, rss, rsr, hss, hsr, wss, wsr, ags, agr, hws, hwr,
    wts, wtr, as_, ar, bs, br, cs, cr, ys, yr,
):
    rows, feats = q_in.shape
    pool = n_in.shape[0]
    wide = PLANE * rows
    lanes = hwb.shape[2]
    chunk = wide // dims
    half = planes // 2
    part = rows // SUB

    b = lax.axis_index("blk")
    e = lax.axis_index("dim")
    z = lax.div(b, PLANE)
    yc = lax.rem(b, PLANE)
    core_yc = yc + 1 - 2 * lax.rem(yc, 2)
    far_yc = lax.rem(yc + 2, PLANE)
    cross_yc = PLANE - 1 - yc

    def at_plane(step):
        return (lax.rem(z + step + planes, planes) * PLANE + yc, e)

    def at_dim(p):
        return (b, lax.rem(e + p, dims))

    core = (z * PLANE + core_yc, e)
    far = (z * PLANE + far_yc, e)
    up, down = at_plane(1), at_plane(-1)

    def take(y, size):
        return pl.ds(pl.multiple_of(y * size, 32), size)

    own = [
        pltpu.make_async_copy(q_in, qbuf.at[0], loc.at[0]),
        pltpu.make_async_copy(p_in, pbuf.at[take(yc, rows)], loc.at[1]),
        pltpu.make_async_copy(n_in, nbuf.at[take(yc, pool)], loc.at[2]),
        pltpu.make_async_copy(idx_in, idxb.at[0], loc.at[3]),
    ]
    for copy in own:
        copy.start()
    barrier = pltpu.get_barrier_semaphore()
    met = [at_plane(s) for s in range(1, planes)] + [core, far]
    met += [at_dim(p) for p in range(1, dims)]
    for device in met:
        pl.semaphore_signal(barrier, inc=1, device_id=device, device_id_type=MESH)
    hp[...] = jnp.zeros_like(hp)
    dnb[...] = jnp.zeros_like(dnb)
    recva[0] = jnp.zeros((rows, feats), BF16)
    recvb[0] = jnp.zeros((rows, feats), BF16)
    for copy in own:
        copy.wait()
    pl.semaphore_wait(barrier, len(met))

    def up_copy(s, i):
        if i == SUB:
            return remote(idxb.at[s - 1], idxb.at[s], us.at[s, i], ur.at[s, i], up)
        at = pl.ds(i * part, part)
        return remote(qbuf.at[s - 1, at], qbuf.at[s, at], us.at[s, i], ur.at[s, i], up)

    def down_copy(s, i):
        src = jnp.where(s == 1, 0, half + s - 1)
        if i == SUB:
            return remote(idxb.at[src], idxb.at[half + s], ds.at[s, i], dr.at[s, i], down)
        at = pl.ds(i * part, part)
        return remote(qbuf.at[src, at], qbuf.at[half + s, at], ds.at[s, i], dr.at[s, i], down)

    def plane_copy(buf, size, sends, recvs, i):
        at = take(far_yc if i == 2 else yc, size)
        return remote(buf.at[at], buf.at[at], sends.at[i], recvs.at[i], far if i == 1 else core)

    p_copy = functools.partial(plane_copy, pbuf, rows, ps, pr)
    n_copy = functools.partial(plane_copy, nbuf, pool, ns, nr)

    for i in range(SUB + 1):
        up_copy(1, i).start()
        down_copy(1, i).start()
    for i in (1, 0):
        p_copy(i).start()
        n_copy(i).start()

    sub = lax.broadcasted_iota(jnp.int32, (8, rows), 0)

    def named(j):
        ids = idxb[j, :, 0:rows] - z * (PLANE * pool)
        low, high = ids & 7, ids >> 3
        keys = [jnp.where(low[k : k + 1] == sub, high[k : k + 1], -1) for k in range(HARD)]
        return ids, keys

    def hard_copy(j):
        step = jnp.where(j <= half, -j, j - half)
        return remote(hp.at[j], hrecv.at[j], hss.at[j], hsr.at[j], at_plane(step))

    def scored(t):
        s = lax.div(t + 1, 2)
        j = jnp.where(lax.rem(t, 2) == 1, s, jnp.where(t == 0, 0, half + s))
        query = qbuf[j]
        ids, keys = named(j)

        def one(y, acc):
            scores = dot(nbuf[take(y, pool)], query, 1, 1)
            base = y * (pool // 8)
            acc = list(acc)
            for r in range(pool // 8):
                tile = scores[8 * r : 8 * r + 8]
                for k in range(HARD):
                    acc[k] = jnp.where(keys[k] == base + r, tile, acc[k])
            return tuple(acc)

        acc = lax.fori_loop(0, PLANE, one, (jnp.zeros((8, rows), F32),) * HARD)
        out = jnp.zeros((8, rows), F32)
        for k in range(HARD):
            out = jnp.where(sub == k, jnp.sum(acc[k], axis=0, keepdims=True), out)
        hp[j, :, 0:rows] = out

        @pl.when(j > 0)
        def _():
            hard_copy(j).start()

    def score_copy(p):
        at = take(lax.rem(e + p, dims), chunk)
        return remote(st.at[at], rbuf.at[p], rss.at[p], rsr.at[p], at_dim(p))

    def version(y):
        return jnp.where(y >= yc, 0, 1)

    def window_scores():
        qcat[0, 0:rows] = qbuf[0]
        qcat[1, 0:rows] = qbuf[REACH]
        for v in range(2):
            for g in range(1, REACH):
                qcat[v, g * rows : (g + 1) * rows] = qbuf[g]

        def one(y):
            at = take(y, rows)
            st[at] = dot(pbuf[at], qcat[version(y)], 1, 1)

        loop(0, PLANE, one)
        for p in range(1, dims):
            score_copy(p).start()

    first, jobs = (3, 3) if half >= 8 else (1, 2)

    def ring_step(s):
        for i in range(SUB + 1):
            up_copy(s, i).wait_recv()

            @pl.when(s < half)
            def _():
                up_copy(s + 1, i).start()
                down_copy(s, i).wait_recv()

            @pl.when(s < half - 1)
            def _():
                down_copy(s + 1, i).start()

        @pl.when(s == first)
        def _():
            for copy in (p_copy, n_copy):
                copy(1).wait_recv()
                copy(2).start()
            for copy in (n_copy, p_copy):
                copy(0).wait_recv()
                copy(2).wait_recv()

        @pl.when(s == REACH)
        def _():
            window_scores()

        @pl.when(s >= first)
        def _():
            low = jobs * (s - first)
            loop(low, jnp.minimum(low + jobs, planes), scored)

    loop(1, half + 1, ring_step)

    total = st[take(e, chunk)]
    for p in range(1, dims):
        score_copy(p).wait_recv()
        total = total + rbuf[p]
    total = total * scale
    sc[...] = total
    top = jnp.max(total, axis=0, keepdims=True)
    part_lse = top + jnp.log(jnp.sum(jnp.exp(total - top), axis=0, keepdims=True))
    part_lse = jnp.broadcast_to(part_lse, (8, wide))
    owner = lax.div(e * chunk, rows)
    ahead = jnp.full((8, lanes), owner, jnp.int32) >= yc

    def lse_copy(g):
        return remote(wsend.at[g], wrecv.at[g], wss.at[g], wsr.at[g], at_plane(-g))

    wsend[0] = jnp.where(ahead, part_lse[:, :lanes], LOW)
    wsend[REACH] = jnp.where(ahead, LOW, part_lse[:, :lanes])
    for g in range(1, REACH):
        wsend[g] = pltpu.roll(part_lse, wide - g * rows, 1)[:, :lanes]
    for g in range(REACH, 0, -1):
        lse_copy(g).start()

    hard_sum = hp[0]
    for j in range(1, planes):
        hard_copy(j).wait_recv()
        hard_sum = hard_sum + hrecv[j]
    parts = [wsend[0]]
    for g in range(1, REACH + 1):
        lse_copy(g).wait_recv()
        parts.append(wrecv[g])

    def joined(values):
        highest = functools.reduce(jnp.maximum, values)
        return highest + jnp.log(sum(jnp.exp(value - highest) for value in values))

    last = lax.broadcasted_iota(jnp.int32, (8, lanes), 0) == HARD
    msg[...] = jnp.where(last, joined(parts), hard_sum)

    def sum_copy(p):
        return remote(msg, arecv.at[p], ags.at[p], agr.at[p], at_dim(p))

    for p in range(1, dims):
        sum_copy(p).start()
    values = [msg[...]]
    for p in range(1, dims):
        sum_copy(p).wait_recv()
        values.append(arecv[p])
    entries = jnp.where(last, joined(values), sum(values) * scale)
    highest = jnp.max(entries, axis=0, keepdims=True)
    log_total = highest + jnp.log(jnp.sum(jnp.exp(entries - highest), axis=0, keepdims=True))
    hard_weights = jnp.exp(entries - log_total).astype(BF16).astype(F32)
    hwb[0] = jnp.where(last, log_total, hard_weights)

    def weight_copy(j):
        step = jnp.where(j <= half, j, half - j)
        return remote(hwb.at[0], hwb.at[j], hws.at[j], hwr.at[j], at_plane(step))

    loop(1, planes, lambda j: weight_copy(j).start())

    lane = lax.broadcasted_iota(jnp.int32, (8, wide), 1)
    logs = jnp.zeros((8, wide), F32)
    for g in range(REACH):
        if g == 0:
            weight_copy(REACH).wait_recv()
            one_log = jnp.where(ahead, hwb[0, HARD : HARD + 1], hwb[REACH, HARD : HARD + 1])
        else:
            weight_copy(g).wait_recv()
            one_log = jnp.broadcast_to(hwb[g, HARD : HARD + 1], (8, lanes))
        if wide > lanes:
            one_log = jnp.concatenate([one_log, jnp.zeros((8, wide - lanes), F32)], axis=1)
        if g > 0:
            one_log = pltpu.roll(one_log, g * rows, 1)
        logs = jnp.where((lane >= g * rows) & (lane < (g + 1) * rows), one_log, logs)
    row_at = lax.broadcasted_iota(jnp.int32, (chunk, wide), 0) + lax.rem(e * chunk, rows)
    lane_at = lax.broadcasted_iota(jnp.int32, (chunk, wide), 1)
    positive = (row_at == lane_at) & (jnp.full((chunk, wide), owner, jnp.int32) == yc)
    weights = jnp.exp(sc[...] - logs[0:1]) - jnp.where(positive, 1.0, 0.0)
    wt[take(e, chunk)] = weights.astype(BF16)

    def tile_copy(p):
        at = take(e, chunk)
        return remote(wt.at[at], wt.at[at], wts.at[p], wtr.at[p], at_dim(p))

    for p in range(1, dims):
        tile_copy(p).start()

    def graded(u):
        t = lax.div(u, 2)
        j = jnp.where(lax.rem(u, 2) == 0, half - t, planes - 1 - t)
        j = jnp.where(u == planes - 1, 0, j)

        @pl.when(j > REACH)
        def _():
            weight_copy(j).wait_recv()

        query = qbuf[j]
        ids, keys = named(j)
        pay = hwb[j, :, 0:rows]
        merged = []
        for k in range(HARD):
            same = jnp.where(ids == ids[k : k + 1], pay, 0.0)
            same = jnp.where(sub < HARD, same, 0.0)
            merged.append(jnp.broadcast_to(jnp.sum(same, axis=0, keepdims=True), (8, rows)))

        def one(y):
            base = y * (pool // 8)
            for r in range(pool // 16):
                pair = []
                for i in range(2):
                    tile = jnp.zeros((8, rows), F32)
                    for k in range(HARD):
                        tile = jnp.where(keys[k] == base + (2 * r + i), merged[k], tile)
                    pair.append(tile)
                at = pl.ds(pl.multiple_of(y * pool + 16 * r, 16), 16)
                wht[at] = jnp.concatenate(pair, axis=0).astype(BF16)
            at = take(y, pool)
            dnb[at] += dot(wht[at], query, 1, 0)

        loop(0, PLANE, one)
        cbuf[j] = dot(wht[...], nbuf[...], 0, 0)

    def window_grads():
        for p in range(1, dims):
            tile_copy(p).wait_recv()
        near = jnp.zeros((lanes, feats), F32)
        rest = jnp.zeros((lanes, feats), F32)
        for y in range(PLANE):
            at = pl.ds(y * rows, rows)
            dpb[at] = dot(wt[at], qcat[version(y)], 1, 0)
            piece = dot(wt[at, 0:lanes], pbuf[at], 0, 0)
            here = jnp.full((lanes, feats), y, jnp.int32) >= yc
            near = near + jnp.where(here, piece, 0.0)
            rest = rest + jnp.where(here, 0.0, piece)
        win[0:lanes] = near + rest
        win[0:rows] = near[0:rows]
        win[REACH * rows : (REACH + 1) * rows] = rest[0:rows]
        if wide > lanes:
            win[lanes:wide] = dot(wt[:, lanes:wide], pbuf[...], 0, 0)

    def a_copy(t):
        return remote(senda.at[t], recva.at[t + 1], as_.at[t + 1], ar.at[t + 1], down)

    def b_copy(t):
        return remote(sendb.at[t], recvb.at[t + 1], bs.at[t + 1], br.at[t + 1], up)

    c_copy = remote(csend, crecv, cs.at[0], cr.at[0], core)
    y_copy = remote(ysend, yrecv, ys.at[0], yr.at[0], far)

    def core_stage():
        for i, y in enumerate((core_yc, cross_yc)):
            csend[i, 0:pool] = dnb[take(y, pool)].astype(BF16)
            csend[i, pool : pool + rows] = dpb[take(y, rows)].astype(BF16)
        c_copy.start()

    def far_stage():
        c_copy.wait_recv()
        ysend[0:pool] = (dnb[take(far_yc, pool)] + crecv[1, 0:pool].astype(F32)).astype(BF16)
        other = dpb[take(far_yc, rows)] + crecv[1, pool : pool + rows].astype(F32)
        ysend[pool : pool + rows] = other.astype(BF16)
        y_copy.start()

    done_at = -(-(planes - 5) // 3)

    def back_step(t):
        ja = half - t

        @pl.when(t > 0)
        def _():
            a_copy(t - 1).wait_recv()

        @pl.when(ja > REACH)
        def _():
            senda[t] = (cbuf[ja] + recva[t].astype(F32)).astype(BF16)

        @pl.when(ja <= REACH)
        def _():
            piece = cbuf[ja] + win[take(ja, rows)]
            senda[t] = (piece + recva[t].astype(F32)).astype(BF16)

        a_copy(t).start()

        @pl.when(t < half - 1)
        def _():
            @pl.when(t > 0)
            def _():
                b_copy(t - 1).wait_recv()

            sendb[t] = (cbuf[planes - 1 - t] + recvb[t].astype(F32)).astype(BF16)
            b_copy(t).start()

        loop(jnp.minimum(2 + 3 * t, planes), jnp.minimum(5 + 3 * t, planes), graded)
        if half > REACH:
            pl.when(t == half - REACH - 1)(window_grads)
        pl.when(t == done_at)(core_stage)
        pl.when(t == done_at + 1)(far_stage)

    loop(0, 2, graded)
    if half <= REACH:
        window_grads()
    loop(0, half, back_step)

    a_copy(half - 1).wait_recv()
    b_copy(half - 2).wait_recv()
    back = recva[half].astype(F32) + recvb[half - 1].astype(F32)
    gq_out[...] = (cbuf[0] + win[0:rows] + back) * scale
    y_copy.wait_recv()
    back = crecv[0].astype(F32) + yrecv[...].astype(F32)
    dn_out[...] = (dnb[take(yc, pool)] + back[0:pool]) * scale
    dp_out[...] = (dpb[take(yc, rows)] + back[pool : pool + rows]) * scale

    for i in range(SUB + 1):
        loop(1, half + 1, lambda s: up_copy(s, i).wait_send())
        loop(1, half, lambda s: down_copy(s, i).wait_send())
    for i in range(3):
        p_copy(i).wait_send()
        n_copy(i).wait_send()
    for p in range(1, dims):
        score_copy(p).wait_send()
        sum_copy(p).wait_send()
        tile_copy(p).wait_send()
    for g in range(1, REACH + 1):
        lse_copy(g).wait_send()
    loop(1, planes, lambda j: hard_copy(j).wait_send())
    loop(1, planes, lambda j: weight_copy(j).wait_send())
    loop(0, half, lambda t: a_copy(t).wait_send())
    loop(0, half - 1, lambda t: b_copy(t).wait_send())
    c_copy.wait_send()
    y_copy.wait_send()


def on_device(queries, passages, negatives, hard_index):
    rows, feats = queries.shape
    pool = negatives.shape[0]
    planes = lax.axis_size("blk") // PLANE
    dims = lax.axis_size("dim")
    half = planes // 2
    wide = PLANE * rows
    chunk = wide // dims
    lanes = -(-rows // 128) * 128
    both = pool + rows
    index = jnp.pad(hard_index.T, ((0, 8 - HARD), (0, lanes - rows)), constant_values=-1)

    dma = pltpu.SemaphoreType.DMA
    vmem = pltpu.VMEM
    scratch = [
        vmem((planes, rows, feats), BF16),
        vmem((planes, 8, lanes), jnp.int32),
        vmem((wide, feats), BF16),
        vmem((PLANE * pool, feats), BF16),
        vmem((2, wide, feats), BF16),
        vmem((wide, wide), F32),
        vmem((dims, chunk, wide), F32),
        vmem((chunk, wide), F32),
        vmem((planes, 8, lanes), F32),
        vmem((planes, 8, lanes), F32),
        vmem((REACH + 1, 8, lanes), F32),
        vmem((REACH + 1, 8, lanes), F32),
        vmem((8, lanes), F32),
        vmem((dims, 8, lanes), F32),
        vmem((planes, 8, lanes), F32),
        vmem((wide, wide), BF16),
        vmem((PLANE * pool, rows), BF16),
        vmem((planes, rows, feats), F32),
        vmem(((REACH + 1) * rows, feats), F32),
        vmem((PLANE * pool, feats), F32),
        vmem((wide, feats), F32),
        vmem((half + 1, rows, feats), BF16),
        vmem((half, rows, feats), BF16),
        vmem((half, rows, feats), BF16),
        vmem((half - 1, rows, feats), BF16),
        vmem((2, both, feats), BF16),
        vmem((2, both, feats), BF16),
        vmem((both, feats), BF16),
        vmem((both, feats), BF16),
        dma((4,)),
    ]
    for shape in (
        (half + 1, SUB + 1), (half, SUB + 1), (3,), (3,), (dims,), (planes,), (REACH + 1,),
        (dims,), (planes,), (dims,), (half + 1,), (half,), (1,), (1,),
    ):
        scratch += [dma(shape), dma(shape)]

    return pl.pallas_call(
        functools.partial(kernel, planes, dims),
        out_shape=(
            jax.ShapeDtypeStruct((rows, feats), F32),
            jax.ShapeDtypeStruct((rows, feats), F32),
            jax.ShapeDtypeStruct((pool, feats), F32),
        ),
        in_specs=[pl.BlockSpec(memory_space=pl.ANY)] * 4,
        out_specs=[pl.BlockSpec(memory_space=pltpu.VMEM)] * 3,
        scratch_shapes=scratch,
        compiler_params=pltpu.CompilerParams(
            collective_id=0, has_side_effects=True, vmem_limit_bytes=60 * 1024 * 1024
        ),
    )(queries, passages, negatives, index)


def solution(mesh):
    placed = (P("blk", "dim"), P("blk", "dim"), P("blk", "dim"), P("blk", None))
    return jax.shard_map(
        on_device,
        mesh=mesh,
        in_specs=placed,
        out_specs=(P("blk", "dim"), P("blk", "dim"), P("blk", "dim")),
        check_vma=False,
    )
```

```python
import functools

import jax
import jax.numpy as jnp
from jax import lax
from jax.experimental import pallas as pl
from jax.experimental.pallas import tpu as pltpu
from jax.sharding import PartitionSpec as P

WINDOW = 16
HARD = 7
PLANE = 4
DIM_Y = 2
REACH = WINDOW // PLANE
SUB = 2
LOW = -1e30

logit_divisor = 0.02
scale = 1.0 / logit_divisor

F32, BF16 = jnp.float32, jnp.bfloat16
MESH = pl.DeviceIdType.MESH


def dot(left, right, left_dim, right_dim):
    return lax.dot_general(
        left, right, (((left_dim,), (right_dim,)), ((), ())), preferred_element_type=F32
    )


def remote(src, dst, send_sem, recv_sem, device):
    return pltpu.make_async_remote_copy(
        src_ref=src,
        dst_ref=dst,
        send_sem=send_sem,
        recv_sem=recv_sem,
        device_id=device,
        device_id_type=MESH,
    )


def loop(low, high, body):
    def step(index, carry):
        body(index)
        return carry

    lax.fori_loop(low, high, step, 0)


def kernel(
    planes, dims,
    q_in, p_in, n_in, idx_in, gq_out, dp_out, dn_out,
    qbuf, idxb, idxp, pbuf, nbuf, qcat, st, relay, merged, nextto, mine, ysum, yget, sc,
    hp, hrecv, wsend, wrecv, msg, arecv, hwb, wt, wht, cbuf, win, dnb, dpb,
    recva, recvb, senda, sendb, nsend, nrecv, psend, precv, nfar, ngot, pfar, pgot,
    loc, us, ur, ds, dr, ps, pr, ns, nr, xs, xr, ls, lr, hss, hsr, wss, wsr, ags, agr,
    hws, hwr, wts, wtr, as_, ar, bs, br, cs, cr, ys, yr,
):
    rows, feats = q_in.shape
    pool = n_in.shape[0]
    wide = PLANE * rows
    two = 2 * rows
    lanes = hwb.shape[2]
    chunk = wide // dims
    half = planes // 2
    part = rows // SUB
    groups = planes // PLANE
    mid = SUB // 2
    across = dims // DIM_Y

    b = lax.axis_index("blk")
    e = lax.axis_index("dim")
    z = lax.div(b, PLANE)
    yc = lax.rem(b, PLANE)
    xx, yy = lax.rem(e, across), lax.div(e, across)
    core_yc = yc + 1 - 2 * lax.rem(yc, 2)
    far_yc = lax.rem(yc + 2, PLANE)
    cross_yc = PLANE - 1 - yc

    def at_plane(step):
        return (lax.rem(z + step + planes, planes) * PLANE + yc, e)

    def at_dim(p):
        return (b, lax.rem(e + p, dims))

    def at_x(step):
        return (b, yy * across + lax.rem(xx + step + across, across))

    core = (z * PLANE + core_yc, e)
    far = (z * PLANE + far_yc, e)
    other_y = at_dim(across)
    up, down = at_plane(1), at_plane(-1)

    def take(y, size, most=32):
        return pl.ds(pl.multiple_of(y * size, most), size)

    def slot_up(s):
        return jnp.maximum(planes - 1 - 2 * s, 0)

    def slot_down(s):
        return jnp.where(s == 0, planes - 1, planes - 2 * s)

    def span(u):
        return jnp.where(lax.rem(u, 2) == 1, -lax.div(planes - 1 - u, 2), lax.div(planes - u, 2))

    mine_slot = planes - 1
    behind = [mine_slot] + [max(planes - 1 - 2 * s, 0) for s in range(1, REACH + 1)]

    own = [
        pltpu.make_async_copy(q_in, qbuf.at[take(mine_slot, rows)], loc.at[0]),
        pltpu.make_async_copy(p_in, pbuf.at[take(yc, rows)], loc.at[1]),
        pltpu.make_async_copy(n_in, nbuf.at[take(yc, pool)], loc.at[2]),
        pltpu.make_async_copy(idx_in, idxb.at[mine_slot], loc.at[3]),
    ]
    for copy in own:
        copy.start()
    barrier = pltpu.get_barrier_semaphore()
    met = [at_plane(s) for s in range(1, planes)] + [core, far]
    met += [at_dim(p) for p in range(1, dims)]
    for device in met:
        pl.semaphore_signal(barrier, inc=1, device_id=device, device_id_type=MESH)
    dnb[...] = jnp.zeros_like(dnb)
    cbuf[...] = jnp.zeros_like(cbuf)
    recva[0] = jnp.zeros((rows, feats), BF16)
    recvb[0] = jnp.zeros((rows, feats), BF16)
    recva[1, mid * part : rows] = jnp.zeros((rows - mid * part, feats), BF16)
    recvb[1, 0 : mid * part] = jnp.zeros((mid * part, feats), BF16)
    for copy in own:
        copy.wait()
    pl.semaphore_wait(barrier, len(met))

    def up_copy(s, i):
        src, dst = slot_up(s - 1), slot_up(s)
        if i == SUB:
            return remote(idxb.at[src], idxb.at[dst], us.at[s, i], ur.at[s, i], up)
        src, dst = (pl.ds(pl.multiple_of(u * rows + i * part, 32), part) for u in (src, dst))
        return remote(qbuf.at[src], qbuf.at[dst], us.at[s, i], ur.at[s, i], up)

    def down_copy(s, i):
        src, dst = slot_down(s - 1), slot_down(s)
        if i == SUB:
            return remote(idxb.at[src], idxb.at[dst], ds.at[s, i], dr.at[s, i], down)
        src, dst = (pl.ds(pl.multiple_of(u * rows + i * part, 32), part) for u in (src, dst))
        return remote(qbuf.at[src], qbuf.at[dst], ds.at[s, i], dr.at[s, i], down)

    def last_up(i):
        return half if i < mid or i == SUB else half - 1

    def last_down(i):
        return half if mid <= i < SUB else half - 1

    def plane_copy(buf, size, sends, recvs, i):
        at = take(far_yc if i == 2 else yc, size)
        return remote(buf.at[at], buf.at[at], sends.at[i], recvs.at[i], far if i == 1 else core)

    p_copy = functools.partial(plane_copy, pbuf, rows, ps, pr)
    n_copy = functools.partial(plane_copy, nbuf, pool, ns, nr)

    p_copy(1).start()
    p_copy(0).start()
    for i in [SUB, *range(SUB)]:
        up_copy(1, i).start()
        down_copy(1, i).start()
    n_copy(1).start()
    n_copy(0).start()

    def beside(values):
        total = None
        width = len(values) * rows
        lane = lax.broadcasted_iota(jnp.int32, (8, width), 1)
        for i, value in enumerate(values):
            if width > lanes:
                fill = jnp.zeros((8, width - lanes), value.dtype)
                value = jnp.concatenate([value, fill], axis=1)
            if i == 0:
                total = value
            else:
                total = jnp.where(lane >= i * rows, pltpu.roll(value, i * rows, 1), total)
        return total

    def hard_copy(u):
        return remote(hp.at[u], hrecv.at[u], hss.at[u], hsr.at[u], at_plane(span(u)))

    sub = lax.broadcasted_iota(jnp.int32, (8, two), 0)

    def scored(p):
        pair = half - 1 - p
        query = qbuf[take(pair, two)]
        ids = beside([idxb[2 * pair], idxb[2 * pair + 1]]) - z * (PLANE * pool)
        idxp[pair] = ids
        low, high = ids & 7, ids >> 3
        keys = [jnp.where(low[k : k + 1] == sub, high[k : k + 1], -1) for k in range(HARD)]

        def one(y, acc):
            scores = dot(nbuf[take(y, pool)], query, 1, 1)
            base = y * (pool // 8)
            acc = list(acc)
            for r in range(pool // 8):
                tile = scores[8 * r : 8 * r + 8]
                for k in range(HARD):
                    acc[k] = jnp.where(keys[k] == base + r, tile, acc[k])
            return tuple(acc)

        acc = lax.fori_loop(0, PLANE, one, (jnp.zeros((8, two), F32),) * HARD)
        out = jnp.zeros((8, two), F32)
        for k in range(HARD):
            out = jnp.where(sub == k, jnp.sum(acc[k], axis=0, keepdims=True), out)
        hp[2 * pair] = out[:, :lanes]
        hp[2 * pair + 1] = pltpu.roll(out, rows, 1)[:, :lanes]
        hard_copy(2 * pair).start()

        @pl.when(p > 0)
        def _():
            hard_copy(2 * pair + 1).start()

    def version(y):
        return jnp.where(y >= yc, 0, 1)

    upper, lower = pl.ds(0, chunk), pl.ds(chunk, chunk)

    def block(step):
        return lax.rem(xx + step + across, across) * two // 2

    def x_copy(h, kind):
        sems = (xs.at[h, kind], xr.at[h, kind])
        ahead_at, behind_at, opposite = block(1), block(-1), block(2)

        def rows_of(start, second):
            return st.at[h, pl.ds(pl.multiple_of(start + second * chunk, 32), chunk)]

        if kind == 0:
            return remote(rows_of(opposite, 0), relay.at[h, 0], *sems, at_x(1))
        if kind == 1:
            return remote(rows_of(opposite, 1), relay.at[h, 1], *sems, at_x(-1))
        if kind == 2:
            return remote(rows_of(ahead_at, 1), nextto.at[h, 0, lower], *sems, at_x(1))
        if kind == 3:
            return remote(rows_of(behind_at, 0), nextto.at[h, 1, upper], *sems, at_x(-1))
        if kind == 4:
            return remote(merged.at[h, 0], nextto.at[h, 0, upper], *sems, at_x(1))
        return remote(merged.at[h, 1], nextto.at[h, 1, lower], *sems, at_x(-1))

    def y_copy(h):
        return remote(ysum.at[h], yget.at[h], ls.at[h], lr.at[h], other_y)

    owner = xx
    ahead = jnp.full((8, lanes), owner, jnp.int32) >= yc

    def lse_copy(g):
        return remote(wsend.at[g], wrecv.at[g], wss.at[g], wsr.at[g], at_plane(-g))

    def window_stage(h, stage):
        if stage == 0:
            if h == 0:
                for i, g in enumerate((1, 2)):
                    for v in range(2):
                        qcat[v, i * rows : (i + 1) * rows] = qbuf[take(behind[g], rows)]
            else:
                for v, g in enumerate((0, REACH)):
                    qcat[v, two : two + rows] = qbuf[take(behind[3], rows)]
                    qcat[v, two + rows : wide] = qbuf[take(behind[g], rows)]

            def one(y):
                at = take(y, rows)
                st[h, at] = dot(pbuf[at], qcat[version(y), h * two : (h + 1) * two], 1, 1)

            loop(0, PLANE, one)
            for kind in range(4):
                x_copy(h, kind).start()
        elif stage == 1:
            for side, start in ((0, block(1)), (1, block(-1))):
                x_copy(h, side).wait_recv()
                at = pl.ds(pl.multiple_of(start + side * chunk, 32), chunk)
                merged[h, side] = st[h, at] + relay[h, side]
                x_copy(h, 4 + side).start()
        elif stage == 2:
            for kind in range(2, 6):
                x_copy(h, kind).wait_recv()
            for keep, start in ((True, yy), (False, 1 - yy)):
                inner = take(start, chunk)
                at = pl.ds(pl.multiple_of(block(0) + start * chunk, 32), chunk)
                total = st[h, at] + nextto[h, 0, inner] + nextto[h, 1, inner]
                if keep:
                    mine[h] = total
                else:
                    ysum[h] = total
            y_copy(h).start()
        else:
            y_copy(h).wait_recv()
            total = (mine[h] + yget[h]) * scale
            sc[h] = total
            top = jnp.max(total, axis=0, keepdims=True)
            lse = top + jnp.log(jnp.sum(jnp.exp(total - top), axis=0, keepdims=True))
            lse = jnp.broadcast_to(lse, (8, two))
            one, another = lse[:, :lanes], pltpu.roll(lse, rows, 1)[:, :lanes]
            if h == 0:
                wsend[1] = one
                wsend[2] = another
                lse_copy(2).start()
                lse_copy(1).start()
            else:
                wsend[3] = one
                wsend[0] = jnp.where(ahead, another, LOW)
                wsend[REACH] = jnp.where(ahead, LOW, another)
                lse_copy(REACH).start()
                lse_copy(3).start()

    first = half // 2

    def ring_step(s):
        for i in [SUB, *range(SUB)]:
            up_last, down_last = last_up(i), last_down(i)

            @pl.when(s <= up_last)
            def _():
                up_copy(s, i).wait_recv()

            @pl.when(s < up_last)
            def _():
                up_copy(s + 1, i).start()

            @pl.when(s <= down_last)
            def _():
                down_copy(s, i).wait_recv()

            @pl.when(s < down_last)
            def _():
                down_copy(s + 1, i).start()

        @pl.when(s == 1)
        def _():
            p_copy(1).wait_recv()
            p_copy(2).start()

        @pl.when(s == 2)
        def _():
            p_copy(0).wait_recv()
            p_copy(2).wait_recv()

        for stage in (3, 2, 1, 0):
            for h in range(2):
                if 2 * h + 2 + stage <= half:
                    pl.when(s == 2 * h + 2 + stage)(functools.partial(window_stage, h, stage))

        @pl.when(s == first)
        def _():
            n_copy(1).wait_recv()
            n_copy(2).start()
            n_copy(0).wait_recv()
            n_copy(2).wait_recv()

        @pl.when(s >= first)
        def _():
            low = jnp.where(s == first, 0, jnp.minimum(2 * (s - first), s - 1))
            loop(low, jnp.minimum(2 * (s - first) + 2, s), scored)

    loop(1, half + 1, ring_step)
    for stage in range(4):
        for h in range(2):
            if 2 * h + 2 + stage > half:
                window_stage(h, stage)

    parts = [wsend[0]]
    for g in range(1, REACH + 1):
        lse_copy(g).wait_recv()
        parts.append(wrecv[g])

    def joined(values):
        highest = functools.reduce(jnp.maximum, values)
        return highest + jnp.log(sum(jnp.exp(value - highest) for value in values))

    window_lse = joined(parts)
    hard_sum = hp[mine_slot]
    for u in range(planes - 2, -1, -1):
        hard_copy(u).wait_recv()
        hard_sum = hard_sum + hrecv[u]
    last = lax.broadcasted_iota(jnp.int32, (8, lanes), 0) == HARD
    msg[...] = jnp.where(last, window_lse, hard_sum)

    def sum_copy(p):
        return remote(msg, arecv.at[p], ags.at[p], agr.at[p], at_dim(p))

    for p in range(1, dims):
        sum_copy(p).start()
    values = [msg[...]]
    for p in range(1, dims):
        sum_copy(p).wait_recv()
        values.append(arecv[p])
    entries = jnp.where(last, joined(values), sum(values) * scale)
    highest = jnp.max(entries, axis=0, keepdims=True)
    log_total = highest + jnp.log(jnp.sum(jnp.exp(entries - highest), axis=0, keepdims=True))
    hard_weights = jnp.exp(entries - log_total).astype(BF16).astype(F32)
    hwb[mine_slot] = jnp.where(last, log_total, hard_weights)

    def weight_copy(u):
        device = at_plane(-span(u))
        return remote(hwb.at[mine_slot], hwb.at[u], hws.at[u], hwr.at[u], device)

    loop(0, planes - 1, lambda u: weight_copy(u).start())

    logs = [jnp.broadcast_to(hwb[mine_slot, HARD : HARD + 1], (8, lanes))]
    for g in range(1, REACH + 1):
        weight_copy(behind[g]).wait_recv()
        logs.append(jnp.broadcast_to(hwb[behind[g], HARD : HARD + 1], (8, lanes)))
    halves = [beside(logs[1:3]), beside([logs[3], jnp.where(ahead, logs[0], logs[REACH])])]
    row_at = lax.broadcasted_iota(jnp.int32, (chunk, two), 0) + yy * chunk + rows
    lane_at = lax.broadcasted_iota(jnp.int32, (chunk, two), 1)
    positive = (row_at == lane_at) & (jnp.full((chunk, two), owner, jnp.int32) == yc)
    my_tile = take(xx * DIM_Y + yy, chunk)
    wt[my_tile, 0:two] = jnp.exp(sc[0] - halves[0][0:1]).astype(BF16)
    weights = jnp.exp(sc[1] - halves[1][0:1]) - jnp.where(positive, 1.0, 0.0)
    wt[my_tile, two:wide] = weights.astype(BF16)

    def tile_copy(p):
        return remote(wt.at[my_tile], wt.at[my_tile], wts.at[p], wtr.at[p], at_dim(p))

    for p in range(1, dims):
        tile_copy(p).start()

    def graded(g):
        for i in range(PLANE):
            u = PLANE * g + i
            fresh = functools.reduce(jnp.logical_and, [u != v for v in behind])

            @pl.when(fresh)
            def _():
                weight_copy(u).wait_recv()

        ids = jnp.concatenate([idxp[2 * g], idxp[2 * g + 1]], axis=1)
        pay = beside([hwb[PLANE * g + i] for i in range(PLANE)])
        counted = lax.broadcasted_iota(jnp.int32, (8, wide), 0) < HARD
        high = ids >> 4
        high = jnp.where((high >= 0) & (high < PLANE * pool // 16), high, -1)
        low = ids & 15
        deep = lax.broadcasted_iota(jnp.int32, (16, wide), 0)
        keys, held = [], []
        for k in range(HARD):
            same = jnp.where((ids == ids[k : k + 1]) & counted, pay, 0.0)
            same = jnp.sum(same, axis=0, keepdims=True)
            held.append(jnp.broadcast_to(same, (16, wide)).astype(BF16))
            key = jnp.where(low[k : k + 1] == deep, high[k : k + 1], -1)
            keys.append(key.astype(F32).astype(BF16))

        for c in range(wide // 128):
            cut = slice(c * 128, (c + 1) * 128)
            key_cut = [key[:, cut] for key in keys]
            held_cut = [value[:, cut] for value in held]

            def one(r):
                base = jnp.full((16, 128), 8 * r, jnp.int32).astype(F32).astype(BF16)
                moved = [key - base for key in key_cut]
                for i in range(8):
                    tile = jnp.zeros((16, 128), BF16)
                    for k in range(HARD):
                        tile = jnp.where(moved[k] == jnp.bfloat16(i), held_cut[k], tile)
                    wht[pl.ds(pl.multiple_of(128 * r + 16 * i, 16), 16), cut] = tile

            loop(0, PLANE * pool // 128, one)

        query = qbuf[take(g, wide)]

        def grown(y):
            at = take(y, pool)
            dnb[at] += dot(wht[at], query, 1, 0)

        loop(0, PLANE, grown)
        cbuf[take(g, wide)] += dot(wht[...], nbuf[...], 0, 0)

    def window_grads():
        for p in range(1, dims):
            tile_copy(p).wait_recv()
        tail = wide - lanes
        near = jnp.zeros((lanes, feats), F32)
        rest = jnp.zeros((lanes, feats), F32)
        for y in range(PLANE):
            at = pl.ds(y * rows, rows)
            dpb[at] = dot(wt[at], qcat[version(y)], 1, 0)
            piece = dot(wt[at, tail:wide], pbuf[at], 0, 0)
            here = jnp.full((lanes, feats), y, jnp.int32) >= yc
            near = near + jnp.where(here, piece, 0.0)
            rest = rest + jnp.where(here, 0.0, piece)
        win[0:tail] = dot(wt[:, 0:tail], pbuf[...], 0, 0)
        win[tail:wide] = near + rest
        for g in range(1, REACH):
            cbuf[take(behind[g], rows)] += win[(g - 1) * rows : g * rows]
        cbuf[take(mine_slot, rows)] += near[lanes - rows : lanes]
        cbuf[take(behind[REACH], rows)] += rest[lanes - rows : lanes]

    def a_copy(t, i):
        at = pl.ds(i * part, part)
        sems = (as_.at[t + 1, i], ar.at[t + 1, i])
        return remote(senda.at[t, at], recva.at[t + 1, at], *sems, down)

    def b_copy(t, i):
        at = pl.ds(i * part, part)
        sems = (bs.at[t + 1, i], br.at[t + 1, i])
        return remote(sendb.at[t, at], recvb.at[t + 1, at], *sems, up)

    def first_a(i):
        return 0 if i < mid else 1

    def first_b(i):
        return 1 - first_a(i)

    def core_copy(kind):
        src, dst = ((nsend, nrecv), (psend, precv))[kind]
        return remote(src, dst, cs.at[kind], cr.at[kind], core)

    def far_copy(kind):
        src, dst = ((nfar, ngot), (pfar, pgot))[kind]
        return remote(src, dst, ys.at[kind], yr.at[kind], far)

    def core_stage(kind):
        total, size, send = ((dnb, pool, nsend), (dpb, rows, psend))[kind]
        for i, y in enumerate((core_yc, cross_yc)):
            send[i] = total[take(y, size)].astype(BF16)
        core_copy(kind).start()

    def far_stage(kind):
        total, size, got, send = ((dnb, pool, nrecv, nfar), (dpb, rows, precv, pfar))[kind]
        core_copy(kind).wait_recv()
        send[...] = (total[take(far_yc, size)] + got[1].astype(F32)).astype(BF16)
        far_copy(kind).start()

    window_at = half - REACH - 1

    def back_step(t):
        ua, ub = jnp.maximum(2 * t - 1, 0), 2 * t
        for i in range(SUB):
            for begin, u, copy, got, send in (
                (first_a(i), ua, a_copy, recva, senda),
                (first_b(i), ub, b_copy, recvb, sendb),
            ):

                @pl.when(t > begin)
                def _():
                    copy(t - 1, i).wait_recv()

                @pl.when(t >= begin)
                def _():
                    at = pl.ds(i * part, part)
                    piece = cbuf[pl.ds(pl.multiple_of(u * rows + i * part, 32), part)]
                    send[t, at] = (piece + got[t, at].astype(F32)).astype(BF16)
                    copy(t, i).start()

        @pl.when(t < groups - 1)
        def _():
            graded(t + 1)

        pl.when(t == groups - 2)(functools.partial(core_stage, 0))
        pl.when(t == groups - 1)(functools.partial(far_stage, 0))
        if window_at >= 0:

            @pl.when(t == window_at)
            def _():
                window_grads()
                core_stage(1)

        pl.when(t == max(window_at, 0) + 1)(functools.partial(far_stage, 1))

    loop(0, 1, graded)
    if window_at < 0:
        window_grads()
        core_stage(1)
    loop(0, half, back_step)

    for kind, total, size, got, crossed, out in (
        (0, dnb, pool, nrecv, ngot, dn_out),
        (1, dpb, rows, precv, pgot, dp_out),
    ):
        far_copy(kind).wait_recv()
        back = got[0].astype(F32) + crossed[...].astype(F32)
        out[...] = (total[take(yc, size)] + back) * scale
    for i in range(SUB):
        a_copy(half - 1, i).wait_recv()
        b_copy(half - 1, i).wait_recv()
    back = recva[half].astype(F32) + recvb[half].astype(F32)
    gq_out[...] = (cbuf[take(mine_slot, rows)] + back) * scale

    for i in range(SUB + 1):
        loop(1, last_up(i) + 1, lambda s: up_copy(s, i).wait_send())
        loop(1, last_down(i) + 1, lambda s: down_copy(s, i).wait_send())
    for i in range(3):
        p_copy(i).wait_send()
        n_copy(i).wait_send()
    for h in range(2):
        for kind in range(6):
            x_copy(h, kind).wait_send()
        y_copy(h).wait_send()
    for p in range(1, dims):
        sum_copy(p).wait_send()
        tile_copy(p).wait_send()
    for g in range(1, REACH + 1):
        lse_copy(g).wait_send()
    loop(0, planes - 1, lambda u: hard_copy(u).wait_send())
    loop(0, planes - 1, lambda u: weight_copy(u).wait_send())
    for i in range(SUB):
        loop(first_a(i), half, lambda t: a_copy(t, i).wait_send())
        loop(first_b(i), half, lambda t: b_copy(t, i).wait_send())
    for kind in range(2):
        core_copy(kind).wait_send()
        far_copy(kind).wait_send()


def on_device(queries, passages, negatives, hard_index):
    rows, feats = queries.shape
    pool = negatives.shape[0]
    planes = lax.axis_size("blk") // PLANE
    dims = lax.axis_size("dim")
    half = planes // 2
    wide, two = PLANE * rows, 2 * rows
    chunk = wide // dims
    lanes = -(-rows // 128) * 128
    index = jnp.pad(hard_index.T, ((0, 8 - HARD), (0, lanes - rows)), constant_values=-1)

    dma = pltpu.SemaphoreType.DMA
    vmem = pltpu.VMEM
    scratch = [
        vmem((planes * rows, feats), BF16),
        vmem((planes, 8, lanes), jnp.int32),
        vmem((half, 8, two), jnp.int32),
        vmem((wide, feats), BF16),
        vmem((PLANE * pool, feats), BF16),
        vmem((2, wide, feats), BF16),
        vmem((2, wide, two), F32),
        vmem((2, 2, chunk, two), F32),
        vmem((2, 2, chunk, two), F32),
        vmem((2, 2, 2 * chunk, two), F32),
        vmem((2, chunk, two), F32),
        vmem((2, chunk, two), F32),
        vmem((2, chunk, two), F32),
        vmem((2, chunk, two), F32),
        vmem((planes, 8, lanes), F32),
        vmem((planes, 8, lanes), F32),
        vmem((REACH + 1, 8, lanes), F32),
        vmem((REACH + 1, 8, lanes), F32),
        vmem((8, lanes), F32),
        vmem((dims, 8, lanes), F32),
        vmem((planes, 8, lanes), F32),
        vmem((wide, wide), BF16),
        vmem((PLANE * pool, wide), BF16),
        vmem((planes * rows, feats), F32),
        vmem((wide, feats), F32),
        vmem((PLANE * pool, feats), F32),
        vmem((wide, feats), F32),
        vmem((half + 1, rows, feats), BF16),
        vmem((half + 1, rows, feats), BF16),
        vmem((half, rows, feats), BF16),
        vmem((half, rows, feats), BF16),
        vmem((2, pool, feats), BF16),
        vmem((2, pool, feats), BF16),
        vmem((2, rows, feats), BF16),
        vmem((2, rows, feats), BF16),
        vmem((pool, feats), BF16),
        vmem((pool, feats), BF16),
        vmem((rows, feats), BF16),
        vmem((rows, feats), BF16),
        dma((4,)),
    ]
    for shape in (
        (half + 1, SUB + 1), (half + 1, SUB + 1), (3,), (3,), (2, 6), (2,), (planes,), (REACH + 1,),
        (dims,), (planes,), (dims,), (half + 1, SUB), (half + 1, SUB), (2,), (2,),
    ):
        scratch += [dma(shape), dma(shape)]

    return pl.pallas_call(
        functools.partial(kernel, planes, dims),
        out_shape=(
            jax.ShapeDtypeStruct((rows, feats), F32),
            jax.ShapeDtypeStruct((rows, feats), F32),
            jax.ShapeDtypeStruct((pool, feats), F32),
        ),
        in_specs=[pl.BlockSpec(memory_space=pl.ANY)] * 4,
        out_specs=[pl.BlockSpec(memory_space=pltpu.VMEM)] * 3,
        scratch_shapes=scratch,
        compiler_params=pltpu.CompilerParams(
            collective_id=0, has_side_effects=True, vmem_limit_bytes=50 * 1024 * 1024
        ),
    )(queries, passages, negatives, index)


def solution(mesh):
    placed = (P("blk", "dim"), P("blk", "dim"), P("blk", "dim"), P("blk", None))
    return jax.shard_map(
        on_device,
        mesh=mesh,
        in_specs=placed,
        out_specs=(P("blk", "dim"), P("blk", "dim"), P("blk", "dim")),
        check_vma=False,
    )
```

```python
import functools

import jax
import jax.numpy as jnp
from jax import lax
from jax.experimental import pallas as pl
from jax.experimental.pallas import tpu as pltpu
from jax.sharding import PartitionSpec as P

WINDOW = 16
HARD = 7
PLANE = 4
DIM_Y = 2
REACH = WINDOW // PLANE
SUB = 2
LOW = -1e30

logit_divisor = 0.02
scale = 1.0 / logit_divisor

F32, BF16 = jnp.float32, jnp.bfloat16
MESH = pl.DeviceIdType.MESH


def dot(left, right, left_dim, right_dim):
    return lax.dot_general(
        left, right, (((left_dim,), (right_dim,)), ((), ())), preferred_element_type=F32
    )


def remote(src, dst, send_sem, recv_sem, device):
    return pltpu.make_async_remote_copy(
        src_ref=src,
        dst_ref=dst,
        send_sem=send_sem,
        recv_sem=recv_sem,
        device_id=device,
        device_id_type=MESH,
    )


def loop(low, high, body):
    def step(index, carry):
        body(index)
        return carry

    lax.fori_loop(low, high, step, 0)


def kernel(
    planes, dims,
    q_in, p_in, n_in, idx_in, gq_out, dp_out, dn_out,
    qbuf, idxb, idxp, pbuf, nbuf, qcat, st, relay, merged, nextto, mine, ysum, yget, sc,
    hpair, hp, hrecv, wsend, wrecv, msg, arecv, hwb, wt, wht, cbuf, win, dnb, dpb,
    recva, recvb, senda, sendb, nsend, nrecv, psend, precv, nfar, ngot, pfar, pgot,
    loc, us, ur, ds, dr, ps, pr, ns, nr, xs, xr, ls, lr, hss, hsr, wss, wsr, ags, agr,
    hws, hwr, wts, wtr, as_, ar, bs, br, cs, cr, ys, yr,
):
    rows, feats = q_in.shape
    pool = n_in.shape[0]
    wide = PLANE * rows
    two = 2 * rows
    lanes = hwb.shape[2]
    chunk = wide // dims
    half = planes // 2
    part = rows // SUB
    groups = planes // PLANE
    mid = SUB // 2
    across = dims // DIM_Y

    b = lax.axis_index("blk")
    e = lax.axis_index("dim")
    z = lax.div(b, PLANE)
    yc = lax.rem(b, PLANE)
    xx, yy = lax.rem(e, across), lax.div(e, across)
    core_yc = yc + 1 - 2 * lax.rem(yc, 2)
    far_yc = lax.rem(yc + 2, PLANE)
    cross_yc = PLANE - 1 - yc

    def at_plane(step):
        return (lax.rem(z + step + planes, planes) * PLANE + yc, e)

    def at_dim(p):
        return (b, lax.rem(e + p, dims))

    def at_x(step):
        return (b, yy * across + lax.rem(xx + step + across, across))

    core = (z * PLANE + core_yc, e)
    far = (z * PLANE + far_yc, e)
    other_y = at_dim(across)
    up, down = at_plane(1), at_plane(-1)

    def take(y, size, most=32):
        return pl.ds(pl.multiple_of(y * size, most), size)

    def slot_up(s):
        return jnp.maximum(planes - 1 - 2 * s, 0)

    def slot_down(s):
        return jnp.where(s == 0, planes - 1, planes - 2 * s)

    def span(u):
        return jnp.where(lax.rem(u, 2) == 1, -lax.div(planes - 1 - u, 2), lax.div(planes - u, 2))

    mine_slot = planes - 1
    behind = [mine_slot] + [max(planes - 1 - 2 * s, 0) for s in range(1, REACH + 1)]

    own = [
        pltpu.make_async_copy(q_in, qbuf.at[take(mine_slot, rows)], loc.at[0]),
        pltpu.make_async_copy(p_in, pbuf.at[take(yc, rows)], loc.at[1]),
        pltpu.make_async_copy(n_in, nbuf.at[take(yc, pool)], loc.at[2]),
        pltpu.make_async_copy(idx_in, idxb.at[mine_slot], loc.at[3]),
    ]
    for copy in own:
        copy.start()
    barrier = pltpu.get_barrier_semaphore()
    met = [at_plane(s) for s in range(1, planes)] + [core, far]
    met += [at_dim(p) for p in range(1, dims)]
    for device in met:
        pl.semaphore_signal(barrier, inc=1, device_id=device, device_id_type=MESH)
    for copy in own:
        copy.wait()
    pl.semaphore_wait(barrier, len(met))

    def up_copy(s, i):
        src, dst = slot_up(s - 1), slot_up(s)
        if i == SUB:
            return remote(idxb.at[src], idxb.at[dst], us.at[s, i], ur.at[s, i], up)
        src, dst = (pl.ds(pl.multiple_of(u * rows + i * part, 32), part) for u in (src, dst))
        return remote(qbuf.at[src], qbuf.at[dst], us.at[s, i], ur.at[s, i], up)

    def down_copy(s, i):
        src, dst = slot_down(s - 1), slot_down(s)
        if i == SUB:
            return remote(idxb.at[src], idxb.at[dst], ds.at[s, i], dr.at[s, i], down)
        src, dst = (pl.ds(pl.multiple_of(u * rows + i * part, 32), part) for u in (src, dst))
        return remote(qbuf.at[src], qbuf.at[dst], ds.at[s, i], dr.at[s, i], down)

    def last_up(i):
        return half if i < mid or i == SUB else half - 1

    def last_down(i):
        return half if mid <= i < SUB else half - 1

    def plane_copy(buf, size, sends, recvs, i):
        at = take(far_yc if i == 2 else yc, size)
        return remote(buf.at[at], buf.at[at], sends.at[i], recvs.at[i], far if i == 1 else core)

    p_copy = functools.partial(plane_copy, pbuf, rows, ps, pr)
    n_copy = functools.partial(plane_copy, nbuf, pool, ns, nr)

    p_copy(1).start()
    p_copy(0).start()
    for i in [SUB, *range(SUB)]:
        up_copy(1, i).start()
        down_copy(1, i).start()
    n_copy(0).start()
    n_copy(1).start()
    dnb[...] = jnp.zeros_like(dnb)
    cbuf[...] = jnp.zeros_like(cbuf)
    recva[0] = jnp.zeros((rows, feats), BF16)
    recvb[0] = jnp.zeros((rows, feats), BF16)
    recva[1, mid * part : rows] = jnp.zeros((rows - mid * part, feats), BF16)
    recvb[1, 0 : mid * part] = jnp.zeros((mid * part, feats), BF16)

    def beside(values):
        total = None
        width = len(values) * rows
        lane = lax.broadcasted_iota(jnp.int32, (8, width), 1)
        for i, value in enumerate(values):
            if width > lanes:
                fill = jnp.zeros((8, width - lanes), value.dtype)
                value = jnp.concatenate([value, fill], axis=1)
            if i == 0:
                total = value
            else:
                total = jnp.where(lane >= i * rows, pltpu.roll(value, i * rows, 1), total)
        return total

    def hard_copy(u):
        return remote(hp.at[u], hrecv.at[u], hss.at[u], hsr.at[u], at_plane(span(u)))

    chip = 2 * lax.div(yc, 2)

    def scored(p, across_y):
        pair = half - 1 - p
        query = qbuf[take(pair, two)]
        begin = jnp.where(across_y == 1, 2 - chip, chip)

        @pl.when(across_y == 0)
        def _():
            ids = beside([idxb[2 * pair], idxb[2 * pair + 1]])
            idxp[pair] = ids - z * (PLANE * pool)
            hpair[pair] = jnp.zeros((8, two), F32)

        low, high = idxp[pair] & 7, idxp[pair] >> 3

        def one(i, acc):
            scores = dot(nbuf[take(begin + i, pool)], query, 1, 1)
            base = (begin + i) * (pool // 8)
            for r in range(pool // 8):
                tile = scores[8 * r : 8 * r + 8]
                picked = jnp.take_along_axis(tile, low, axis=0, mode="promise_in_bounds")
                acc = jnp.where(high == base + r, picked, acc)
            return acc

        out = lax.fori_loop(0, 2, one, hpair[pair])
        hpair[pair] = out

        @pl.when(across_y == 1)
        def _():
            hp[2 * pair] = out[:, :lanes]
            hp[2 * pair + 1] = pltpu.roll(out, rows, 1)[:, :lanes]
            hard_copy(2 * pair).start()

            @pl.when(p > 0)
            def _():
                hard_copy(2 * pair + 1).start()

    def version(y):
        return jnp.where(y >= yc, 0, 1)

    upper, lower = pl.ds(0, chunk), pl.ds(chunk, chunk)

    def block(step):
        return lax.rem(xx + step + across, across) * two // 2

    def x_copy(h, kind):
        sems = (xs.at[h, kind], xr.at[h, kind])
        ahead_at, behind_at, opposite = block(1), block(-1), block(2)

        def rows_of(start, second):
            return st.at[h, pl.ds(pl.multiple_of(start + second * chunk, 32), chunk)]

        if kind == 0:
            return remote(rows_of(opposite, 0), relay.at[h, 0], *sems, at_x(1))
        if kind == 1:
            return remote(rows_of(opposite, 1), relay.at[h, 1], *sems, at_x(-1))
        if kind == 2:
            return remote(rows_of(ahead_at, 1), nextto.at[h, 0, lower], *sems, at_x(1))
        if kind == 3:
            return remote(rows_of(behind_at, 0), nextto.at[h, 1, upper], *sems, at_x(-1))
        if kind == 4:
            return remote(merged.at[h, 0], nextto.at[h, 0, upper], *sems, at_x(1))
        return remote(merged.at[h, 1], nextto.at[h, 1, lower], *sems, at_x(-1))

    def y_copy(h):
        return remote(ysum.at[h], yget.at[h], ls.at[h], lr.at[h], other_y)

    owner = xx
    ahead = jnp.full((8, lanes), owner, jnp.int32) >= yc

    def lse_copy(g):
        return remote(wsend.at[g], wrecv.at[g], wss.at[g], wsr.at[g], at_plane(-g))

    def window_stage(h, stage):
        if stage == 0:
            if h == 0:
                for i, g in enumerate((1, 2)):
                    for v in range(2):
                        qcat[v, i * rows : (i + 1) * rows] = qbuf[take(behind[g], rows)]
            else:
                for v, g in enumerate((0, REACH)):
                    qcat[v, two : two + rows] = qbuf[take(behind[3], rows)]
                    qcat[v, two + rows : wide] = qbuf[take(behind[g], rows)]

            def one(y):
                at = take(y, rows)
                st[h, at] = dot(pbuf[at], qcat[version(y), h * two : (h + 1) * two], 1, 1)

            loop(0, PLANE, one)
            for kind in range(4):
                x_copy(h, kind).start()
        elif stage == 1:
            for side, start in ((0, block(1)), (1, block(-1))):
                x_copy(h, side).wait_recv()
                at = pl.ds(pl.multiple_of(start + side * chunk, 32), chunk)
                merged[h, side] = st[h, at] + relay[h, side]
                x_copy(h, 4 + side).start()
        elif stage == 2:
            for kind in range(2, 6):
                x_copy(h, kind).wait_recv()
            for keep, start in ((True, yy), (False, 1 - yy)):
                inner = take(start, chunk)
                at = pl.ds(pl.multiple_of(block(0) + start * chunk, 32), chunk)
                total = st[h, at] + nextto[h, 0, inner] + nextto[h, 1, inner]
                if keep:
                    mine[h] = total
                else:
                    ysum[h] = total
            y_copy(h).start()
        else:
            y_copy(h).wait_recv()
            total = (mine[h] + yget[h]) * scale
            sc[h] = total
            top = jnp.max(total, axis=0, keepdims=True)
            lse = top + jnp.log(jnp.sum(jnp.exp(total - top), axis=0, keepdims=True))
            lse = jnp.broadcast_to(lse, (8, two))
            one, another = lse[:, :lanes], pltpu.roll(lse, rows, 1)[:, :lanes]
            if h == 0:
                wsend[1] = one
                wsend[2] = another
                lse_copy(2).start()
                lse_copy(1).start()
            else:
                wsend[3] = one
                wsend[0] = jnp.where(ahead, another, LOW)
                wsend[REACH] = jnp.where(ahead, LOW, another)
                lse_copy(REACH).start()
                lse_copy(3).start()

    first = half // 2
    jobs, left = [], list(range(half))
    for s in range(1, half + 1):
        early = 0 if s < first else 2 if s == half else 1
        jobs.append([(left.pop(0), 1) for _ in range(early) if left and left[0] <= s - 2])
        jobs.append([(s - 1, 0)])
        if s == first:
            jobs[-1] += [(left.pop(0), 1)]
    jobs[-1] += [(p, 1) for p in left]
    queue = sum(jobs, [])

    def lookup(index, values):
        found = jnp.int32(values[0])
        for i, value in enumerate(values):
            found = jnp.where(index >= i, value, found)
        return found

    ends = [sum(len(some) for some in jobs[: i + 1]) for i in range(len(jobs))]

    def queued(q):
        scored(lookup(q, [p for p, _ in queue]), lookup(q, [kind for _, kind in queue]))

    stage_at = {0: 0, 1: 1, 2: 3, 3: 4}

    def ring_step(s):
        for i in [SUB, *range(SUB)]:
            up_last, down_last = last_up(i), last_down(i)

            @pl.when(s <= up_last)
            def _():
                up_copy(s, i).wait_recv()

            @pl.when(s < up_last)
            def _():
                up_copy(s + 1, i).start()

            @pl.when(s <= down_last)
            def _():
                down_copy(s, i).wait_recv()

            @pl.when(s < down_last)
            def _():
                down_copy(s + 1, i).start()

            if i == SUB:
                continue
            if i == 0:

                @pl.when(s == 1)
                def _():
                    n_copy(0).wait_recv()

                @pl.when(s == 2)
                def _():
                    p_copy(0).wait_recv()
                    p_copy(2).wait_recv()

                @pl.when(s == first)
                def _():
                    n_copy(1).wait_recv()
                    n_copy(2).start()
                    n_copy(2).wait_recv()

            if i < 2:
                slot = 2 * (s - 1) + i
                low = jnp.where(slot == 0, 0, lookup(slot - 1, ends))
                loop(low, lookup(slot, ends), queued)

        @pl.when(s == 1)
        def _():
            p_copy(1).wait_recv()
            p_copy(2).start()

        for stage in (3, 2, 1, 0):
            for h in range(2):
                step = 2 * h + 2 + stage_at[stage]
                if step <= half:
                    pl.when(s == step)(functools.partial(window_stage, h, stage))

    loop(1, half + 1, ring_step)
    for stage in range(4):
        for h in range(2):
            if 2 * h + 2 + stage_at[stage] > half:
                window_stage(h, stage)

    parts = [wsend[0]]
    for g in range(1, REACH + 1):
        lse_copy(g).wait_recv()
        parts.append(wrecv[g])

    def joined(values):
        highest = functools.reduce(jnp.maximum, values)
        return highest + jnp.log(sum(jnp.exp(value - highest) for value in values))

    window_lse = joined(parts)
    hard_sum = hp[mine_slot]
    for u in range(planes - 2, -1, -1):
        hard_copy(u).wait_recv()
        hard_sum = hard_sum + hrecv[u]
    last = lax.broadcasted_iota(jnp.int32, (8, lanes), 0) == HARD
    msg[...] = jnp.where(last, window_lse, hard_sum)

    def sum_copy(p):
        return remote(msg, arecv.at[p], ags.at[p], agr.at[p], at_dim(p))

    for p in range(1, dims):
        sum_copy(p).start()
    values = [msg[...]]
    for p in range(1, dims):
        sum_copy(p).wait_recv()
        values.append(arecv[p])
    entries = jnp.where(last, joined(values), sum(values) * scale)
    highest = jnp.max(entries, axis=0, keepdims=True)
    log_total = highest + jnp.log(jnp.sum(jnp.exp(entries - highest), axis=0, keepdims=True))
    hard_weights = jnp.exp(entries - log_total).astype(BF16).astype(F32)
    hwb[mine_slot] = jnp.where(last, log_total, hard_weights)

    def weight_copy(u):
        device = at_plane(-span(u))
        return remote(hwb.at[mine_slot], hwb.at[u], hws.at[u], hwr.at[u], device)

    loop(0, planes - 1, lambda u: weight_copy(u).start())

    logs = [jnp.broadcast_to(hwb[mine_slot, HARD : HARD + 1], (8, lanes))]
    for g in range(1, REACH + 1):
        weight_copy(behind[g]).wait_recv()
        logs.append(jnp.broadcast_to(hwb[behind[g], HARD : HARD + 1], (8, lanes)))
    halves = [beside(logs[1:3]), beside([logs[3], jnp.where(ahead, logs[0], logs[REACH])])]
    row_at = lax.broadcasted_iota(jnp.int32, (chunk, two), 0) + yy * chunk + rows
    lane_at = lax.broadcasted_iota(jnp.int32, (chunk, two), 1)
    positive = (row_at == lane_at) & (jnp.full((chunk, two), owner, jnp.int32) == yc)
    my_tile = take(xx * DIM_Y + yy, chunk)
    wt[my_tile, 0:two] = jnp.exp(sc[0] - halves[0][0:1]).astype(BF16)
    weights = jnp.exp(sc[1] - halves[1][0:1]) - jnp.where(positive, 1.0, 0.0)
    wt[my_tile, two:wide] = weights.astype(BF16)

    def tile_copy(p):
        return remote(wt.at[my_tile], wt.at[my_tile], wts.at[p], wtr.at[p], at_dim(p))

    for p in range(1, dims):
        tile_copy(p).start()

    def graded(g):
        for i in range(PLANE):
            u = PLANE * g + i
            fresh = functools.reduce(jnp.logical_and, [u != v for v in behind])

            @pl.when(fresh)
            def _():
                weight_copy(u).wait_recv()

        ids = jnp.concatenate([idxp[2 * g], idxp[2 * g + 1]], axis=1)
        pay = beside([hwb[PLANE * g + i] for i in range(PLANE)])
        counted = lax.broadcasted_iota(jnp.int32, (8, wide), 0) < HARD
        high = ids >> 4
        high = jnp.where((high >= 0) & (high < PLANE * pool // 16), high, -1)
        low = ids & 15
        deep = lax.broadcasted_iota(jnp.int32, (16, wide), 0)
        keys, held = [], []
        for k in range(HARD):
            same = jnp.where((ids == ids[k : k + 1]) & counted, pay, 0.0)
            same = jnp.sum(same, axis=0, keepdims=True)
            held.append(jnp.broadcast_to(same, (16, wide)).astype(BF16))
            key = jnp.where(low[k : k + 1] == deep, high[k : k + 1], -1)
            keys.append(key.astype(F32).astype(BF16))

        for c in range(wide // 128):
            cut = slice(c * 128, (c + 1) * 128)
            key_cut = [key[:, cut] for key in keys]
            held_cut = [value[:, cut] for value in held]

            def one(r):
                base = jnp.full((16, 128), 8 * r, jnp.int32).astype(F32).astype(BF16)
                moved = [key - base for key in key_cut]
                for i in range(8):
                    tile = jnp.zeros((16, 128), BF16)
                    for k in range(HARD):
                        tile = jnp.where(moved[k] == jnp.bfloat16(i), held_cut[k], tile)
                    wht[pl.ds(pl.multiple_of(128 * r + 16 * i, 16), 16), cut] = tile

            loop(0, PLANE * pool // 128, one)

    def grown(g):
        query = qbuf[take(g, wide)]

        def one(y):
            at = take(y, pool)
            dnb[at] += dot(wht[at], query, 1, 0)

        loop(0, PLANE, one)
        cbuf[take(g, wide)] += dot(wht[...], nbuf[...], 0, 0)

    def window_grads():
        for p in range(1, dims):
            tile_copy(p).wait_recv()
        tail = wide - lanes
        near = jnp.zeros((lanes, feats), F32)
        rest = jnp.zeros((lanes, feats), F32)
        for y in range(PLANE):
            at = pl.ds(y * rows, rows)
            dpb[at] = dot(wt[at], qcat[version(y)], 1, 0)
            piece = dot(wt[at, tail:wide], pbuf[at], 0, 0)
            here = jnp.full((lanes, feats), y, jnp.int32) >= yc
            near = near + jnp.where(here, piece, 0.0)
            rest = rest + jnp.where(here, 0.0, piece)
        win[0:tail] = dot(wt[:, 0:tail], pbuf[...], 0, 0)
        win[tail:wide] = near + rest
        for g in range(1, REACH):
            cbuf[take(behind[g], rows)] += win[(g - 1) * rows : g * rows]
        cbuf[take(mine_slot, rows)] += near[lanes - rows : lanes]
        cbuf[take(behind[REACH], rows)] += rest[lanes - rows : lanes]

    def a_copy(t, i):
        at = pl.ds(i * part, part)
        sems = (as_.at[t + 1, i], ar.at[t + 1, i])
        return remote(senda.at[t, at], recva.at[t + 1, at], *sems, down)

    def b_copy(t, i):
        at = pl.ds(i * part, part)
        sems = (bs.at[t + 1, i], br.at[t + 1, i])
        return remote(sendb.at[t, at], recvb.at[t + 1, at], *sems, up)

    def first_a(i):
        return 0 if i < mid else 1

    def first_b(i):
        return 1 - first_a(i)

    def core_copy(kind):
        src, dst = ((nsend, nrecv), (psend, precv))[kind]
        return remote(src, dst, cs.at[kind], cr.at[kind], core)

    def far_copy(kind):
        src, dst = ((nfar, ngot), (pfar, pgot))[kind]
        return remote(src, dst, ys.at[kind], yr.at[kind], far)

    def core_stage(kind):
        total, size, send = ((dnb, pool, nsend), (dpb, rows, psend))[kind]
        for i, y in enumerate((core_yc, cross_yc)):
            send[i] = total[take(y, size)].astype(BF16)
        core_copy(kind).start()

    def far_stage(kind):
        total, size, got, send = ((dnb, pool, nrecv, nfar), (dpb, rows, precv, pfar))[kind]
        core_copy(kind).wait_recv()
        send[...] = (total[take(far_yc, size)] + got[1].astype(F32)).astype(BF16)
        far_copy(kind).start()

    window_at = half - REACH - 1

    def back_step(t):
        ua, ub = jnp.maximum(2 * t - 1, 0), 2 * t
        for i in range(SUB):
            for begin, u, copy, got, send in (
                (first_a(i), ua, a_copy, recva, senda),
                (first_b(i), ub, b_copy, recvb, sendb),
            ):

                @pl.when(t > begin)
                def _():
                    copy(t - 1, i).wait_recv()

                @pl.when(t >= begin)
                def _():
                    at = pl.ds(i * part, part)
                    piece = cbuf[pl.ds(pl.multiple_of(u * rows + i * part, 32), part)]
                    send[t, at] = (piece + got[t, at].astype(F32)).astype(BF16)
                    copy(t, i).start()

            if i < 2:
                pl.when(t < groups - 1)(functools.partial((graded, grown)[i], t + 1))

        pl.when(t == groups - 2)(functools.partial(core_stage, 0))
        pl.when(t == groups - 1)(functools.partial(far_stage, 0))
        if window_at >= 0:

            @pl.when(t == window_at)
            def _():
                window_grads()
                core_stage(1)

        pl.when(t == max(window_at, 0) + 1)(functools.partial(far_stage, 1))

    loop(0, 1, graded)
    loop(0, 1, grown)
    if window_at < 0:
        window_grads()
        core_stage(1)
    loop(0, half, back_step)

    for kind, total, size, got, crossed, out in (
        (0, dnb, pool, nrecv, ngot, dn_out),
        (1, dpb, rows, precv, pgot, dp_out),
    ):
        far_copy(kind).wait_recv()
        back = got[0].astype(F32) + crossed[...].astype(F32)
        out[...] = (total[take(yc, size)] + back) * scale
    for i in range(SUB):
        a_copy(half - 1, i).wait_recv()
        b_copy(half - 1, i).wait_recv()
    back = recva[half].astype(F32) + recvb[half].astype(F32)
    gq_out[...] = (cbuf[take(mine_slot, rows)] + back) * scale

    for i in range(SUB + 1):
        loop(1, last_up(i) + 1, lambda s: up_copy(s, i).wait_send())
        loop(1, last_down(i) + 1, lambda s: down_copy(s, i).wait_send())
    for i in range(3):
        p_copy(i).wait_send()
        n_copy(i).wait_send()
    for h in range(2):
        for kind in range(6):
            x_copy(h, kind).wait_send()
        y_copy(h).wait_send()
    for p in range(1, dims):
        sum_copy(p).wait_send()
        tile_copy(p).wait_send()
    for g in range(1, REACH + 1):
        lse_copy(g).wait_send()
    loop(0, planes - 1, lambda u: hard_copy(u).wait_send())
    loop(0, planes - 1, lambda u: weight_copy(u).wait_send())
    for i in range(SUB):
        loop(first_a(i), half, lambda t: a_copy(t, i).wait_send())
        loop(first_b(i), half, lambda t: b_copy(t, i).wait_send())
    for kind in range(2):
        core_copy(kind).wait_send()
        far_copy(kind).wait_send()


def on_device(queries, passages, negatives, hard_index):
    rows, feats = queries.shape
    pool = negatives.shape[0]
    planes = lax.axis_size("blk") // PLANE
    dims = lax.axis_size("dim")
    half = planes // 2
    wide, two = PLANE * rows, 2 * rows
    chunk = wide // dims
    lanes = -(-rows // 128) * 128
    index = jnp.pad(hard_index.T, ((0, 8 - HARD), (0, lanes - rows)), constant_values=-1)

    dma = pltpu.SemaphoreType.DMA
    vmem = pltpu.VMEM
    scratch = [
        vmem((planes * rows, feats), BF16),
        vmem((planes, 8, lanes), jnp.int32),
        vmem((half, 8, two), jnp.int32),
        vmem((wide, feats), BF16),
        vmem((PLANE * pool, feats), BF16),
        vmem((2, wide, feats), BF16),
        vmem((2, wide, two), F32),
        vmem((2, 2, chunk, two), F32),
        vmem((2, 2, chunk, two), F32),
        vmem((2, 2, 2 * chunk, two), F32),
        vmem((2, chunk, two), F32),
        vmem((2, chunk, two), F32),
        vmem((2, chunk, two), F32),
        vmem((2, chunk, two), F32),
        vmem((half, 8, two), F32),
        vmem((planes, 8, lanes), F32),
        vmem((planes, 8, lanes), F32),
        vmem((REACH + 1, 8, lanes), F32),
        vmem((REACH + 1, 8, lanes), F32),
        vmem((8, lanes), F32),
        vmem((dims, 8, lanes), F32),
        vmem((planes, 8, lanes), F32),
        vmem((wide, wide), BF16),
        vmem((PLANE * pool, wide), BF16),
        vmem((planes * rows, feats), F32),
        vmem((wide, feats), F32),
        vmem((PLANE * pool, feats), F32),
        vmem((wide, feats), F32),
        vmem((half + 1, rows, feats), BF16),
        vmem((half + 1, rows, feats), BF16),
        vmem((half, rows, feats), BF16),
        vmem((half, rows, feats), BF16),
        vmem((2, pool, feats), BF16),
        vmem((2, pool, feats), BF16),
        vmem((2, rows, feats), BF16),
        vmem((2, rows, feats), BF16),
        vmem((pool, feats), BF16),
        vmem((pool, feats), BF16),
        vmem((rows, feats), BF16),
        vmem((rows, feats), BF16),
        dma((4,)),
    ]
    for shape in (
        (half + 1, SUB + 1), (half + 1, SUB + 1), (3,), (3,), (2, 6), (2,), (planes,), (REACH + 1,),
        (dims,), (planes,), (dims,), (half + 1, SUB), (half + 1, SUB), (2,), (2,),
    ):
        scratch += [dma(shape), dma(shape)]

    return pl.pallas_call(
        functools.partial(kernel, planes, dims),
        out_shape=(
            jax.ShapeDtypeStruct((rows, feats), F32),
            jax.ShapeDtypeStruct((rows, feats), F32),
            jax.ShapeDtypeStruct((pool, feats), F32),
        ),
        in_specs=[pl.BlockSpec(memory_space=pl.ANY)] * 4,
        out_specs=[pl.BlockSpec(memory_space=pltpu.VMEM)] * 3,
        scratch_shapes=scratch,
        compiler_params=pltpu.CompilerParams(
            collective_id=0, has_side_effects=True, vmem_limit_bytes=50 * 1024 * 1024
        ),
    )(queries, passages, negatives, index)


def solution(mesh):
    placed = (P("blk", "dim"), P("blk", "dim"), P("blk", "dim"), P("blk", None))
    return jax.shard_map(
        on_device,
        mesh=mesh,
        in_specs=placed,
        out_specs=(P("blk", "dim"), P("blk", "dim"), P("blk", "dim")),
        check_vma=False,
    )
```

```python
import functools

import jax
import jax.numpy as jnp
from jax import lax
from jax.experimental import pallas as pl
from jax.experimental.pallas import tpu as pltpu
from jax.sharding import PartitionSpec as P

WINDOW = 16
HARD = 7
PLANE = 4
DIM_Y = 2
REACH = WINDOW // PLANE
SUB = 2
LOW = -1e30

logit_divisor = 0.02
scale = 1.0 / logit_divisor

F32, BF16 = jnp.float32, jnp.bfloat16
MESH = pl.DeviceIdType.MESH


def dot(left, right, left_dim, right_dim):
    return lax.dot_general(
        left, right, (((left_dim,), (right_dim,)), ((), ())), preferred_element_type=F32
    )


def remote(src, dst, send_sem, recv_sem, device):
    return pltpu.make_async_remote_copy(
        src_ref=src,
        dst_ref=dst,
        send_sem=send_sem,
        recv_sem=recv_sem,
        device_id=device,
        device_id_type=MESH,
    )


def loop(low, high, body):
    def step(index, carry):
        body(index)
        return carry

    lax.fori_loop(low, high, step, 0)


def kernel(
    planes, dims,
    q_in, p_in, n_in, idx_in, gq_out, dp_out, dn_out,
    qbuf, idx0, idxb, idxp, pbuf, nbuf, qcat, st, relay, merged, nextto, mine, ysum, yget, sc,
    hpair, hp, hrecv, wsend, wrecv, msg, arecv, hwb, logb, wt, keyb, heldb, wht, cbuf, win, dnb, dpb,
    recva, recvb, senda, sendb, nsend, nrecv, psend, precv, nfar, ngot, pfar, pgot,
    loc, us, ur, ds, dr, ps, pr, ns, nr, xs, xr, ls, lr, hss, hsr, wss, wsr, ags, agr,
    hws, hwr, los, lor, wts, wtr, as_, ar, bs, br, cs, cr, ys, yr,
):
    rows, feats = q_in.shape
    pool = n_in.shape[0]
    wide = PLANE * rows
    two = 2 * rows
    lanes = logb.shape[2]
    chunk = wide // dims
    half = planes // 2
    part = rows // SUB
    groups = planes // PLANE
    mid = SUB // 2
    across = dims // DIM_Y

    b = lax.axis_index("blk")
    e = lax.axis_index("dim")
    z = lax.div(b, PLANE)
    yc = lax.rem(b, PLANE)
    xx, yy = lax.rem(e, across), lax.div(e, across)
    core_yc = yc + 1 - 2 * lax.rem(yc, 2)
    far_yc = lax.rem(yc + 2, PLANE)
    cross_yc = PLANE - 1 - yc

    def at_plane(step):
        return (lax.rem(z + step + planes, planes) * PLANE + yc, e)

    def at_dim(p):
        return (b, lax.rem(e + p, dims))

    def at_x(step):
        return (b, yy * across + lax.rem(xx + step + across, across))

    core = (z * PLANE + core_yc, e)
    far = (z * PLANE + far_yc, e)
    other_y = at_dim(across)
    up, down = at_plane(1), at_plane(-1)

    def take(y, size, most=32):
        return pl.ds(pl.multiple_of(y * size, most), size)

    def slot_up(s):
        return jnp.maximum(planes - 1 - 2 * s, 0)

    def slot_down(s):
        return jnp.where(s == 0, planes - 1, planes - 2 * s)

    def span(u):
        return jnp.where(lax.rem(u, 2) == 1, -lax.div(planes - 1 - u, 2), lax.div(planes - u, 2))

    mine_slot = planes - 1
    behind = [mine_slot] + [max(planes - 1 - 2 * s, 0) for s in range(1, REACH + 1)]

    own = [
        pltpu.make_async_copy(q_in, qbuf.at[take(mine_slot, rows)], loc.at[0]),
        pltpu.make_async_copy(p_in, pbuf.at[take(yc, rows)], loc.at[1]),
        pltpu.make_async_copy(n_in, nbuf.at[take(yc, pool)], loc.at[2]),
        pltpu.make_async_copy(idx_in, idx0, loc.at[3]),
    ]
    for copy in own:
        copy.start()
    barrier = pltpu.get_barrier_semaphore()
    met = [at_plane(s) for s in range(1, planes)] + [core, far]
    met += [at_dim(p) for p in range(1, dims)]
    for device in met:
        pl.semaphore_signal(barrier, inc=1, device_id=device, device_id_type=MESH)
    for copy in own:
        copy.wait()
    idxb[mine_slot] = jnp.full((8, lanes), -1, jnp.int32)
    idxb[mine_slot, 0:HARD, 0:rows] = idx0[...]
    pl.semaphore_wait(barrier, len(met))

    def first_a(i):
        return jnp.where(i < mid, 0, 1) if isinstance(i, jax.Array) else int(i >= mid)

    def first_b(i):
        return 1 - first_a(i)

    def up_copy(s, i):
        src, dst = slot_up(s - 1), slot_up(s)
        if i is SUB:
            return remote(idxb.at[src], idxb.at[dst], us.at[s, i], ur.at[s, i], up)
        src, dst = (pl.ds(pl.multiple_of(u * rows + i * part, 16), part) for u in (src, dst))
        return remote(qbuf.at[src], qbuf.at[dst], us.at[s, i], ur.at[s, i], up)

    def down_copy(s, i):
        src, dst = slot_down(s - 1), slot_down(s)
        if i is SUB:
            return remote(idxb.at[src], idxb.at[dst], ds.at[s, i], dr.at[s, i], down)
        src, dst = (pl.ds(pl.multiple_of(u * rows + i * part, 16), part) for u in (src, dst))
        return remote(qbuf.at[src], qbuf.at[dst], ds.at[s, i], dr.at[s, i], down)

    def last_up(i):
        return half if i is SUB else half - 1 + first_b(i)

    def last_down(i):
        return half - 1 if i is SUB else half - 1 + first_a(i)

    def plane_copy(buf, size, sends, recvs, i):
        at = take(far_yc if i == 2 else yc, size)
        return remote(buf.at[at], buf.at[at], sends.at[i], recvs.at[i], far if i == 1 else core)

    p_copy = functools.partial(plane_copy, pbuf, rows, ps, pr)
    n_copy = functools.partial(plane_copy, nbuf, pool, ns, nr)

    p_copy(1).start()
    p_copy(0).start()
    for i in [SUB, *range(SUB)]:
        up_copy(1, i).start()
        down_copy(1, i).start()
    n_copy(0).start()
    cbuf[...] = jnp.zeros_like(cbuf)
    recva[0] = jnp.zeros((rows, feats), BF16)
    recvb[0] = jnp.zeros((rows, feats), BF16)
    recva[1, mid * part : rows] = jnp.zeros((rows - mid * part, feats), BF16)
    recvb[1, 0 : mid * part] = jnp.zeros((mid * part, feats), BF16)

    def beside(values):
        total = None
        width = len(values) * rows
        lane = lax.broadcasted_iota(jnp.int32, (8, width), 1)
        for i, value in enumerate(values):
            if width > lanes:
                fill = jnp.zeros((8, width - lanes), value.dtype)
                value = jnp.concatenate([value, fill], axis=1)
            if i == 0:
                total = value
            else:
                total = jnp.where(lane >= i * rows, pltpu.roll(value, i * rows, 1), total)
        return total

    def hard_copy(u):
        return remote(hp.at[u], hrecv.at[u], hss.at[u], hsr.at[u], at_plane(span(u)))

    chip = 2 * lax.div(yc, 2)

    def scored(p, across_y):
        pair = half - 1 - p
        query = qbuf[take(pair, two)]
        begin = jnp.where(across_y == 1, 2 - chip, chip)

        @pl.when(across_y == 0)
        def _():
            ids = beside([idxb[2 * pair], idxb[2 * pair + 1]])
            idxp[pair] = ids - z * (PLANE * pool)
            hpair[pair] = jnp.zeros((8, two), F32)

        low, high = idxp[pair] & 7, idxp[pair] >> 3

        def one(i, acc):
            scores = dot(nbuf[take(begin + i, pool)], query, 1, 1)
            base = (begin + i) * (pool // 8)
            for r in range(pool // 8):
                tile = scores[8 * r : 8 * r + 8]
                picked = jnp.take_along_axis(tile, low, axis=0, mode="promise_in_bounds")
                acc = jnp.where(high == base + r, picked, acc)
            return acc

        out = lax.fori_loop(0, 2, one, hpair[pair])
        hpair[pair] = out

        @pl.when(across_y == 1)
        def _():
            hp[2 * pair] = out[:, :lanes]
            hp[2 * pair + 1] = pltpu.roll(out, rows, 1)[:, :lanes]
            hard_copy(2 * pair).start()

            @pl.when(p > 0)
            def _():
                hard_copy(2 * pair + 1).start()

    def version(y):
        return jnp.where(y >= yc, 0, 1)

    upper, lower = pl.ds(0, chunk), pl.ds(chunk, chunk)

    def block(step):
        return lax.rem(xx + step + across, across) * two // 2

    def x_copy(h, kind):
        sems = (xs.at[h, kind], xr.at[h, kind])
        ahead_at, behind_at, opposite = block(1), block(-1), block(2)

        def rows_of(start, second):
            return st.at[h, pl.ds(pl.multiple_of(start + second * chunk, 32), chunk)]

        if kind == 0:
            return remote(rows_of(opposite, 0), relay.at[h, 0], *sems, at_x(1))
        if kind == 1:
            return remote(rows_of(opposite, 1), relay.at[h, 1], *sems, at_x(-1))
        if kind == 2:
            return remote(rows_of(ahead_at, 1), nextto.at[h, 0, lower], *sems, at_x(1))
        if kind == 3:
            return remote(rows_of(behind_at, 0), nextto.at[h, 1, upper], *sems, at_x(-1))
        if kind == 4:
            return remote(merged.at[h, 0], nextto.at[h, 0, upper], *sems, at_x(1))
        return remote(merged.at[h, 1], nextto.at[h, 1, lower], *sems, at_x(-1))

    def y_copy(h):
        return remote(ysum.at[h], yget.at[h], ls.at[h], lr.at[h], other_y)

    owner = xx
    ahead = jnp.full((8, lanes), owner, jnp.int32) >= yc

    def lse_copy(g):
        return remote(wsend.at[g], wrecv.at[g], wss.at[g], wsr.at[g], at_plane(-g))

    def window_stage(h, stage):
        if stage == 0:
            if h == 0:
                for i, g in enumerate((1, 2)):
                    for v in range(2):
                        qcat[v, i * rows : (i + 1) * rows] = qbuf[take(behind[g], rows)]
            else:
                for v, g in enumerate((0, REACH)):
                    qcat[v, two : two + rows] = qbuf[take(behind[3], rows)]
                    qcat[v, two + rows : wide] = qbuf[take(behind[g], rows)]

            def one(y):
                at = take(y, rows)
                st[h, at] = dot(pbuf[at], qcat[version(y), h * two : (h + 1) * two], 1, 1)

            loop(0, PLANE, one)
            for kind in range(2):
                x_copy(h, kind).start()
        elif stage == 1:
            for side, start in ((0, block(1)), (1, block(-1))):
                x_copy(h, side).wait_recv()
                at = pl.ds(pl.multiple_of(start + side * chunk, 32), chunk)
                merged[h, side] = st[h, at] + relay[h, side]
                x_copy(h, 4 + side).start()
            for kind in (2, 3):
                x_copy(h, kind).start()
        elif stage == 2:
            for kind in range(2, 6):
                x_copy(h, kind).wait_recv()
            for keep, start in ((True, yy), (False, 1 - yy)):
                inner = take(start, chunk)
                at = pl.ds(pl.multiple_of(block(0) + start * chunk, 32), chunk)
                total = st[h, at] + nextto[h, 0, inner] + nextto[h, 1, inner]
                if keep:
                    mine[h] = total
                else:
                    ysum[h] = total
            y_copy(h).start()
        else:
            y_copy(h).wait_recv()
            total = (mine[h] + yget[h]) * scale
            sc[h] = total
            top = jnp.max(total, axis=0, keepdims=True)
            lse = top + jnp.log(jnp.sum(jnp.exp(total - top), axis=0, keepdims=True))
            lse = jnp.broadcast_to(lse, (8, two))
            one, another = lse[:, :lanes], pltpu.roll(lse, rows, 1)[:, :lanes]
            if h == 0:
                wsend[1] = one
                wsend[2] = another
                lse_copy(2).start()
                lse_copy(1).start()
            else:
                wsend[3] = one
                wsend[0] = jnp.where(ahead, another, LOW)
                wsend[REACH] = jnp.where(ahead, LOW, another)
                lse_copy(REACH).start()
                lse_copy(3).start()

    first = half // 2
    jobs, left = [], list(range(half))
    for s in range(1, half + 1):
        early = 0 if s < first else 2 if s == half else 1
        jobs.append([(left.pop(0), 1) for _ in range(early) if left and left[0] <= s - 2])
        jobs.append([(s - 1, 0)])
        if s == first:
            jobs[-1] += [(left.pop(0), 1)]
    jobs[-1] += [(p, 1) for p in left]
    queue = sum(jobs, [])

    def lookup(index, values):
        found = jnp.int32(values[0])
        for i, value in enumerate(values):
            found = jnp.where(index >= i, value, found)
        return found

    ends = [sum(len(some) for some in jobs[: i + 1]) for i in range(len(jobs))]

    def queued(q):
        scored(lookup(q, [p for p, _ in queue]), lookup(q, [kind for _, kind in queue]))

    stage_at = {(0, 0): 3, (0, 1): 5, (0, 2): 9, (0, 3): 12, (1, 0): 7, (1, 1): 10, (1, 2): 14}

    def ring_move(s, i):
        up_last, down_last = last_up(i), last_down(i)

        @pl.when(s <= up_last)
        def _():
            up_copy(s, i).wait_recv()

        @pl.when(s < up_last)
        def _():
            up_copy(s + 1, i).start()

        @pl.when(s <= down_last)
        def _():
            down_copy(s, i).wait_recv()

        @pl.when(s < down_last)
        def _():
            down_copy(s + 1, i).start()

    def ring_slot(slot):
        s, i = lax.div(slot, SUB) + 1, lax.rem(slot, SUB)

        @pl.when(i == 0)
        def _():
            ring_move(s, SUB)

        ring_move(s, i)

        @pl.when(slot == 0)
        def _():
            n_copy(0).wait_recv()

        @pl.when(slot == 1)
        def _():
            p_copy(1).wait_recv()
            p_copy(2).start()
            n_copy(1).start()

        @pl.when(slot == 2)
        def _():
            p_copy(0).wait_recv()
            p_copy(2).wait_recv()

        @pl.when(slot == 2 * (first - 1))
        def _():
            n_copy(1).wait_recv()
            n_copy(2).start()
            n_copy(2).wait_recv()

        for (h, stage), when in stage_at.items():
            if stage > 0:
                pl.when(slot == when)(functools.partial(window_stage, h, stage))
        low = jnp.where(slot == 0, 0, lookup(slot - 1, ends))
        loop(low, lookup(slot, ends), queued)
        for (h, stage), when in stage_at.items():
            if stage == 0:
                pl.when(slot == when)(functools.partial(window_stage, h, stage))

    loop(0, SUB * half, ring_slot)
    window_stage(1, 3)

    parts = [wsend[0]]
    for g in range(1, REACH + 1):
        lse_copy(g).wait_recv()
        parts.append(wrecv[g])

    def folded(value):
        cuts = [value[:, c : c + 128] for c in range(0, lanes, 128)]
        return jnp.concatenate(cuts, axis=0).astype(BF16)

    def unfolded(value):
        value = value.astype(F32)
        return jnp.concatenate([value[c : c + 8] for c in range(0, lanes // 16, 8)], axis=1)

    def joined(values):
        highest = functools.reduce(jnp.maximum, values)
        return highest + jnp.log(sum(jnp.exp(value - highest) for value in values))

    window_lse = joined(parts)
    hard_sum = hp[mine_slot]
    for u in range(planes - 2, -1, -1):
        hard_copy(u).wait_recv()
        hard_sum = hard_sum + hrecv[u]
    last = lax.broadcasted_iota(jnp.int32, (8, lanes), 0) == HARD
    msg[...] = jnp.where(last, window_lse, hard_sum)

    def sum_copy(p):
        return remote(msg, arecv.at[p], ags.at[p], agr.at[p], at_dim(p))

    for p in range(1, dims):
        sum_copy(p).start()
    values = [msg[...]]
    for p in range(1, dims):
        sum_copy(p).wait_recv()
        values.append(arecv[p])
    entries = jnp.where(last, joined(values), sum(values) * scale)
    highest = jnp.max(entries, axis=0, keepdims=True)
    log_total = highest + jnp.log(jnp.sum(jnp.exp(entries - highest), axis=0, keepdims=True))
    hard_weights = jnp.exp(entries - log_total)
    hwb[mine_slot] = folded(hard_weights)
    logb[0] = jnp.broadcast_to(log_total, (8, lanes))

    def log_copy(g):
        return remote(logb.at[0], logb.at[g], los.at[g], lor.at[g], at_plane(g))

    def weight_copy(u):
        device = at_plane(-span(u))
        return remote(hwb.at[mine_slot], hwb.at[u], hws.at[u], hwr.at[u], device)

    loop(0, 4, lambda u: weight_copy(u).start())
    for g in range(1, REACH + 1):
        log_copy(g).start()
    loop(4, planes - 1, lambda u: weight_copy(u).start())

    logs = [logb[0]]
    for g in range(1, REACH + 1):
        log_copy(g).wait_recv()
        logs.append(logb[g])
    halves = [beside(logs[1:3]), beside([logs[3], jnp.where(ahead, logs[0], logs[REACH])])]
    row_at = lax.broadcasted_iota(jnp.int32, (chunk, two), 0) + yy * chunk + rows
    lane_at = lax.broadcasted_iota(jnp.int32, (chunk, two), 1)
    positive = (row_at == lane_at) & (jnp.full((chunk, two), owner, jnp.int32) == yc)
    my_tile = take(xx * DIM_Y + yy, chunk)
    wt[my_tile, 0:two] = jnp.exp(sc[0] - halves[0][0:1]).astype(BF16)
    weights = jnp.exp(sc[1] - halves[1][0:1]) - jnp.where(positive, 1.0, 0.0)
    wt[my_tile, two:wide] = weights.astype(BF16)

    def tile_copy(p):
        return remote(wt.at[my_tile], wt.at[my_tile], wts.at[p], wtr.at[p], at_dim(p))

    for p in range(1, dims):
        tile_copy(p).start()

    def graded(g):
        for i in range(PLANE):
            u = PLANE * g + i

            @pl.when(u != mine_slot)
            def _():
                weight_copy(u).wait_recv()

        ids = jnp.concatenate([idxp[2 * g], idxp[2 * g + 1]], axis=1)
        pay = beside([unfolded(hwb[PLANE * g + i]) for i in range(PLANE)])
        counted = lax.broadcasted_iota(jnp.int32, (8, wide), 0) < HARD
        high = ids >> 4
        high = jnp.where((high >= 0) & (high < PLANE * pool // 16), high, -1)
        low = ids & 15
        deep = lax.broadcasted_iota(jnp.int32, (16, wide), 0)
        keys, held = [], []
        for k in range(HARD):
            same = jnp.where((ids == ids[k : k + 1]) & counted, pay, 0.0)
            same = jnp.sum(same, axis=0, keepdims=True)
            held.append(jnp.broadcast_to(same, (16, wide)).astype(BF16))
            key = jnp.where(low[k : k + 1] == deep, high[k : k + 1], -1)
            keys.append(key.astype(F32).astype(BF16))

        for k in range(HARD):
            keyb[k] = keys[k]
            heldb[k] = held[k]

    def built(g):
        def cut_at(c):
            cut = pl.ds(pl.multiple_of(c * 128, 128), 128)
            out = pl.ds(pl.multiple_of(g * wide + c * 128, 128), 128)
            key_cut = [keyb[k, :, cut] for k in range(HARD)]
            held_cut = [heldb[k, :, cut] for k in range(HARD)]

            def one(r):
                base = jnp.full((16, 128), 8 * r, jnp.int32).astype(F32).astype(BF16)
                moved = [key - base for key in key_cut]
                for i in range(8):
                    tile = jnp.zeros((16, 128), BF16)
                    for k in range(HARD):
                        tile = jnp.where(moved[k] == jnp.bfloat16(i), held_cut[k], tile)
                    wht[pl.ds(pl.multiple_of(128 * r + 16 * i, 16), 16), out] = tile

            loop(0, PLANE * pool // 128, one)

        loop(0, wide // 128, cut_at)

    def grown(y):
        at = take(y, pool)
        dnb[at] = dot(wht[at], qbuf[...], 1, 0)

    def returned(g):
        at = pl.ds(pl.multiple_of(g * wide, 128), wide)
        cbuf[take(g, wide)] += dot(wht[:, at], nbuf[...], 0, 0)

    def window_documents():
        def one(y):
            at = take(y, rows)
            dpb[at] = dot(wt[at], qcat[version(y)], 1, 0)

        loop(0, PLANE, one)

    tail = wide - lanes

    def window_queries():
        for p in range(1, dims):
            tile_copy(p).wait_recv()
        win[0:tail] = dot(wt[:, 0:tail], pbuf[...], 0, 0)
        for g in range(1, REACH - 1):
            cbuf[take(behind[g], rows)] += win[(g - 1) * rows : g * rows]

    def window_ends():
        near = jnp.zeros((lanes, feats), F32)
        rest = jnp.zeros((lanes, feats), F32)
        for y in range(PLANE):
            at = pl.ds(y * rows, rows)
            piece = dot(wt[at, tail:wide], pbuf[at], 0, 0)
            here = jnp.full((lanes, feats), y, jnp.int32) >= yc
            near = near + jnp.where(here, piece, 0.0)
            rest = rest + jnp.where(here, 0.0, piece)
        win[tail:wide] = near + rest
        cbuf[take(behind[3], rows)] += win[two:two + rows]
        cbuf[take(mine_slot, rows)] += near[lanes - rows : lanes]
        cbuf[take(behind[REACH], rows)] += rest[lanes - rows : lanes]

    def a_copy(t, i):
        at = pl.ds(pl.multiple_of(i * part, 16), part)
        sems = (as_.at[t + 1, i], ar.at[t + 1, i])
        return remote(senda.at[t, at], recva.at[t + 1, at], *sems, down)

    def b_copy(t, i):
        at = pl.ds(pl.multiple_of(i * part, 16), part)
        sems = (bs.at[t + 1, i], br.at[t + 1, i])
        return remote(sendb.at[t, at], recvb.at[t + 1, at], *sems, up)

    def core_copy(kind):
        src, dst = ((nsend, nrecv), (psend, precv))[kind]
        return remote(src, dst, cs.at[kind], cr.at[kind], core)

    def far_copy(kind):
        src, dst = ((nfar, ngot), (pfar, pgot))[kind]
        return remote(src, dst, ys.at[kind], yr.at[kind], far)

    def core_stage(kind):
        total, size, send = ((dnb, pool, nsend), (dpb, rows, psend))[kind]
        for i, y in enumerate((core_yc, cross_yc)):
            send[i] = total[take(y, size)].astype(BF16)
        core_copy(kind).start()

    def far_stage(kind):
        total, size, got, send = ((dnb, pool, nrecv, nfar), (dpb, rows, precv, pfar))[kind]
        core_copy(kind).wait_recv()
        send[...] = (total[take(far_yc, size)] + got[1].astype(F32)).astype(BF16)
        far_copy(kind).start()

    def back_slot(slot):
        @pl.when(slot >= 1)
        def _():
            t, i = lax.div(slot - 1, SUB), lax.rem(slot - 1, SUB)
            for begin, u, copy, got, send in (
                (first_a(i), jnp.maximum(2 * t - 1, 0), a_copy, recva, senda),
                (first_b(i), 2 * t, b_copy, recvb, sendb),
            ):

                @pl.when(t > begin)
                def _():
                    copy(t - 1, i).wait_recv()

                @pl.when(t >= begin)
                def _():
                    at = pl.ds(pl.multiple_of(i * part, 16), part)
                    piece = cbuf[pl.ds(pl.multiple_of(u * rows + i * part, 16), part)]
                    send[t, at] = (piece + got[t, at].astype(F32)).astype(BF16)
                    copy(t, i).start()

        @pl.when(slot < groups)
        def _():
            graded(slot)
            built(slot)

        @pl.when((slot == 0) | (slot == 4) | (slot == 7) | (slot == 10))
        def _():
            returned(lax.div(slot, 3))

        @pl.when((slot == 5) | (slot == 6))
        def _():
            grown(jnp.where(slot == 5, core_yc, far_yc))
            grown(jnp.where(slot == 5, cross_yc, yc))

        pl.when(slot == 5)(functools.partial(core_stage, 0))
        pl.when(slot == 7)(functools.partial(far_stage, 0))

        @pl.when(slot == 8)
        def _():
            window_queries()
            window_ends()

        @pl.when(slot == 9)
        def _():
            window_documents()
            core_stage(1)

        pl.when(slot == 11)(functools.partial(far_stage, 1))

    loop(0, SUB * half + 1, back_slot)

    for kind, total, size, got, crossed, out in (
        (0, dnb, pool, nrecv, ngot, dn_out),
        (1, dpb, rows, precv, pgot, dp_out),
    ):
        far_copy(kind).wait_recv()
        back = got[0].astype(F32) + crossed[...].astype(F32)
        out[...] = total[take(yc, size)] + back
    for i in range(SUB):
        a_copy(half - 1, i).wait_recv()
        b_copy(half - 1, i).wait_recv()
    back = recva[half].astype(F32) + recvb[half].astype(F32)
    gq_out[...] = cbuf[take(mine_slot, rows)] + back

    for i in range(SUB + 1):
        loop(1, last_up(i) + 1, lambda s: up_copy(s, i).wait_send())
        loop(1, last_down(i) + 1, lambda s: down_copy(s, i).wait_send())
    for i in range(3):
        p_copy(i).wait_send()
        n_copy(i).wait_send()
    for h in range(2):
        for kind in range(6):
            x_copy(h, kind).wait_send()
        y_copy(h).wait_send()
    for p in range(1, dims):
        sum_copy(p).wait_send()
        tile_copy(p).wait_send()
    for g in range(1, REACH + 1):
        lse_copy(g).wait_send()
        log_copy(g).wait_send()
    loop(0, planes - 1, lambda u: hard_copy(u).wait_send())
    loop(0, planes - 1, lambda u: weight_copy(u).wait_send())
    for i in range(SUB):
        loop(first_a(i), half, functools.partial(lambda i, t: a_copy(t, i).wait_send(), i))
        loop(first_b(i), half, lambda t: b_copy(t, i).wait_send())
    for kind in range(2):
        core_copy(kind).wait_send()
        far_copy(kind).wait_send()


def on_device(queries, passages, negatives, hard_index):
    rows, feats = queries.shape
    pool = negatives.shape[0]
    planes = lax.axis_size("blk") // PLANE
    dims = lax.axis_size("dim")
    half = planes // 2
    wide, two = PLANE * rows, 2 * rows
    chunk = wide // dims
    lanes = -(-rows // 128) * 128

    dma = pltpu.SemaphoreType.DMA
    vmem = pltpu.VMEM
    scratch = [
        vmem((planes * rows, feats), BF16),
        vmem((HARD, rows), jnp.int32),
        vmem((planes, 8, lanes), jnp.int32),
        vmem((half, 8, two), jnp.int32),
        vmem((wide, feats), BF16),
        vmem((PLANE * pool, feats), BF16),
        vmem((2, wide, feats), BF16),
        vmem((2, wide, two), F32),
        vmem((2, 2, chunk, two), F32),
        vmem((2, 2, chunk, two), F32),
        vmem((2, 2, 2 * chunk, two), F32),
        vmem((2, chunk, two), F32),
        vmem((2, chunk, two), F32),
        vmem((2, chunk, two), F32),
        vmem((2, chunk, two), F32),
        vmem((half, 8, two), F32),
        vmem((planes, 8, lanes), F32),
        vmem((planes, 8, lanes), F32),
        vmem((REACH + 1, 8, lanes), F32),
        vmem((REACH + 1, 8, lanes), F32),
        vmem((8, lanes), F32),
        vmem((dims, 8, lanes), F32),
        vmem((planes, lanes // 16, 128), BF16),
        vmem((REACH + 1, 8, lanes), F32),
        vmem((wide, wide), BF16),
        vmem((HARD, 16, wide), BF16),
        vmem((HARD, 16, wide), BF16),
        vmem((PLANE * pool, planes * rows), BF16),
        vmem((planes * rows, feats), F32),
        vmem((wide, feats), F32),
        vmem((PLANE * pool, feats), F32),
        vmem((wide, feats), F32),
        vmem((half + 1, rows, feats), BF16),
        vmem((half + 1, rows, feats), BF16),
        vmem((half, rows, feats), BF16),
        vmem((half, rows, feats), BF16),
        vmem((2, pool, feats), BF16),
        vmem((2, pool, feats), BF16),
        vmem((2, rows, feats), BF16),
        vmem((2, rows, feats), BF16),
        vmem((pool, feats), BF16),
        vmem((pool, feats), BF16),
        vmem((rows, feats), BF16),
        vmem((rows, feats), BF16),
        dma((4,)),
    ]
    for shape in (
        (half + 1, SUB + 1), (half + 1, SUB + 1), (3,), (3,), (2, 6), (2,), (planes,), (REACH + 1,),
        (dims,), (planes,), (REACH + 1,), (dims,), (half + 1, SUB), (half + 1, SUB), (2,), (2,),
    ):
        scratch += [dma(shape), dma(shape)]

    sums = pl.pallas_call(
        functools.partial(kernel, planes, dims),
        out_shape=(
            jax.ShapeDtypeStruct((rows, feats), F32),
            jax.ShapeDtypeStruct((rows, feats), F32),
            jax.ShapeDtypeStruct((pool, feats), F32),
        ),
        in_specs=[pl.BlockSpec(memory_space=pltpu.HBM)] * 4,
        out_specs=[pl.BlockSpec(memory_space=pltpu.VMEM)] * 3,
        scratch_shapes=scratch,
        compiler_params=pltpu.CompilerParams(
            collective_id=0, has_side_effects=True, vmem_limit_bytes=60 * 1024 * 1024
        ),
    )(queries, passages, negatives, hard_index.T)
    return tuple(total * scale for total in sums)


def solution(mesh):
    placed = (P("blk", "dim"), P("blk", "dim"), P("blk", "dim"), P("blk", None))
    return jax.shard_map(
        on_device,
        mesh=mesh,
        in_specs=placed,
        out_specs=(P("blk", "dim"), P("blk", "dim"), P("blk", "dim")),
        check_vma=False,
    )
```

```python
import functools

import jax
import jax.numpy as jnp
from jax import lax
from jax.experimental import pallas as pl
from jax.experimental.pallas import tpu as pltpu
from jax.sharding import PartitionSpec as P

WINDOW = 16
HARD = 7
PLANE = 4
DIM_Y = 2
REACH = WINDOW // PLANE
SUB = 2
LOW = -1e30

logit_divisor = 0.02
scale = 1.0 / logit_divisor

F32, BF16 = jnp.float32, jnp.bfloat16
MESH = pl.DeviceIdType.MESH


def dot(left, right, left_dim, right_dim):
    return lax.dot_general(
        left, right, (((left_dim,), (right_dim,)), ((), ())), preferred_element_type=F32
    )


def remote(src, dst, send_sem, recv_sem, device):
    return pltpu.make_async_remote_copy(
        src_ref=src,
        dst_ref=dst,
        send_sem=send_sem,
        recv_sem=recv_sem,
        device_id=device,
        device_id_type=MESH,
    )


def loop(low, high, body):
    def step(index, carry):
        body(index)
        return carry

    lax.fori_loop(low, high, step, 0)


def kernel(
    planes, dims,
    q_in, p_in, n_in, idx_in, gq_out, dp_out, dn_out,
    qbuf, idx0, idxb, idxp, pbuf, nbuf, qcat, st, relay, merged, nextto, mine, ysum, yget, sc,
    hpair, hp, hrecv, wsend, wrecv, msg, arecv, hwb, logb, wt, keyb, heldb, wht, cbuf, win, dnb, dpb,
    recva, recvb, senda, sendb, nsend, nrecv, psend, precv, nfar, ngot, pfar, pgot,
    loc, us, ur, ds, dr, ps, pr, ns, nr, xs, xr, ls, lr, hss, hsr, wss, wsr, ags, agr,
    hws, hwr, los, lor, wts, wtr, as_, ar, bs, br, cs, cr, ys, yr,
):
    rows, feats = q_in.shape
    pool = n_in.shape[0]
    wide = PLANE * rows
    two = 2 * rows
    lanes = logb.shape[2]
    chunk = wide // dims
    half = planes // 2
    part = rows // SUB
    groups = planes // PLANE
    mid = SUB // 2
    across = dims // DIM_Y

    b = lax.axis_index("blk")
    e = lax.axis_index("dim")
    z = lax.div(b, PLANE)
    yc = lax.rem(b, PLANE)
    xx, yy = lax.rem(e, across), lax.div(e, across)
    core_yc = yc + 1 - 2 * lax.rem(yc, 2)
    far_yc = lax.rem(yc + 2, PLANE)
    cross_yc = PLANE - 1 - yc

    def at_plane(step):
        return (lax.rem(z + step + planes, planes) * PLANE + yc, e)

    def at_dim(p):
        return (b, lax.rem(e + p, dims))

    def at_x(step):
        return (b, yy * across + lax.rem(xx + step + across, across))

    core = (z * PLANE + core_yc, e)
    far = (z * PLANE + far_yc, e)
    other_y = at_dim(across)
    up, down = at_plane(1), at_plane(-1)

    def take(y, size, most=32):
        return pl.ds(pl.multiple_of(y * size, most), size)

    def slot_up(s):
        return jnp.maximum(planes - 1 - 2 * s, 0)

    def slot_down(s):
        return jnp.where(s == 0, planes - 1, planes - 2 * s)

    def span(u):
        return jnp.where(lax.rem(u, 2) == 1, -lax.div(planes - 1 - u, 2), lax.div(planes - u, 2))

    mine_slot = planes - 1
    behind = [mine_slot] + [max(planes - 1 - 2 * s, 0) for s in range(1, REACH + 1)]

    own = [
        pltpu.make_async_copy(q_in, qbuf.at[take(mine_slot, rows)], loc.at[0]),
        pltpu.make_async_copy(p_in, pbuf.at[take(yc, rows)], loc.at[1]),
        pltpu.make_async_copy(n_in, nbuf.at[take(yc, pool)], loc.at[2]),
        pltpu.make_async_copy(idx_in, idx0, loc.at[3]),
    ]
    barrier = pltpu.get_barrier_semaphore()
    met = [at_plane(s) for s in range(1, planes)] + [core, far]
    met += [at_dim(p) for p in range(1, dims)]
    for device in met:
        pl.semaphore_signal(barrier, inc=1, device_id=device, device_id_type=MESH)
    for copy in own:
        copy.start()
    for copy in own:
        copy.wait()
    idxb[mine_slot] = jnp.full((8, lanes), -1, jnp.int32)
    idxb[mine_slot, 0:HARD, 0:rows] = idx0[...]
    pl.semaphore_wait(barrier, len(met))

    def first_a(i):
        return jnp.where(i < mid, 0, 1) if isinstance(i, jax.Array) else int(i >= mid)

    def first_b(i):
        return 1 - first_a(i)

    def up_copy(s, i):
        src, dst = slot_up(s - 1), slot_up(s)
        if i is SUB:
            return remote(idxb.at[src], idxb.at[dst], us.at[s, i], ur.at[s, i], up)
        src, dst = (pl.ds(pl.multiple_of(u * rows + i * part, 16), part) for u in (src, dst))
        return remote(qbuf.at[src], qbuf.at[dst], us.at[s, i], ur.at[s, i], up)

    def down_copy(s, i):
        src, dst = slot_down(s - 1), slot_down(s)
        if i is SUB:
            return remote(idxb.at[src], idxb.at[dst], ds.at[s, i], dr.at[s, i], down)
        src, dst = (pl.ds(pl.multiple_of(u * rows + i * part, 16), part) for u in (src, dst))
        return remote(qbuf.at[src], qbuf.at[dst], ds.at[s, i], dr.at[s, i], down)

    def last_up(i):
        return half if i is SUB else half - 1 + first_b(i)

    def last_down(i):
        return half - 1 if i is SUB else half - 1 + first_a(i)

    def plane_copy(buf, size, sends, recvs, i):
        at = take(far_yc if i == 2 else yc, size)
        return remote(buf.at[at], buf.at[at], sends.at[i], recvs.at[i], far if i == 1 else core)

    p_copy = functools.partial(plane_copy, pbuf, rows, ps, pr)
    n_copy = functools.partial(plane_copy, nbuf, pool, ns, nr)

    p_copy(1).start()
    p_copy(0).start()
    for i in [SUB, *range(SUB)]:
        up_copy(1, i).start()
        down_copy(1, i).start()
    n_copy(0).start()
    cbuf[...] = jnp.zeros_like(cbuf)
    recva[0] = jnp.zeros((rows, feats), BF16)
    recvb[0] = jnp.zeros((rows, feats), BF16)
    recva[1, mid * part : rows] = jnp.zeros((rows - mid * part, feats), BF16)
    recvb[1, 0 : mid * part] = jnp.zeros((mid * part, feats), BF16)

    def beside(values):
        total = None
        width = len(values) * rows
        lane = lax.broadcasted_iota(jnp.int32, (8, width), 1)
        for i, value in enumerate(values):
            if width > lanes:
                fill = jnp.zeros((8, width - lanes), value.dtype)
                value = jnp.concatenate([value, fill], axis=1)
            if i == 0:
                total = value
            else:
                total = jnp.where(lane >= i * rows, pltpu.roll(value, i * rows, 1), total)
        return total

    def hard_copy(u):
        return remote(hp.at[u], hrecv.at[u], hss.at[u], hsr.at[u], at_plane(span(u)))

    chip = 2 * lax.div(yc, 2)

    def scored(p, across_y):
        pair = half - 1 - p
        query = qbuf[take(pair, two)]
        begin = jnp.where(across_y == 1, 2 - chip, chip)

        @pl.when(across_y == 0)
        def _():
            ids = beside([idxb[2 * pair], idxb[2 * pair + 1]])
            idxp[pair] = ids - z * (PLANE * pool)
            hpair[pair] = jnp.zeros((8, two), F32)

        low, high = idxp[pair] & 7, idxp[pair] >> 3

        def one(i, acc):
            scores = dot(nbuf[take(begin + i, pool)], query, 1, 1)
            base = (begin + i) * (pool // 8)
            for r in range(pool // 8):
                tile = scores[8 * r : 8 * r + 8]
                picked = jnp.take_along_axis(tile, low, axis=0, mode="promise_in_bounds")
                acc = jnp.where(high == base + r, picked, acc)
            return acc

        out = lax.fori_loop(0, 2, one, hpair[pair])
        hpair[pair] = out

        @pl.when(across_y == 1)
        def _():
            hp[2 * pair] = out[:, :lanes]
            hp[2 * pair + 1] = pltpu.roll(out, rows, 1)[:, :lanes]
            hard_copy(2 * pair).start()

            @pl.when(p > 0)
            def _():
                hard_copy(2 * pair + 1).start()

    def version(y):
        return jnp.where(y >= yc, 0, 1)

    upper, lower = pl.ds(0, chunk), pl.ds(chunk, chunk)

    def block(step):
        return lax.rem(xx + step + across, across) * two // 2

    def x_copy(h, kind):
        sems = (xs.at[h, kind], xr.at[h, kind])
        ahead_at, behind_at, opposite = block(1), block(-1), block(2)

        def rows_of(start, second):
            return st.at[h, pl.ds(pl.multiple_of(start + second * chunk, 32), chunk)]

        if kind == 0:
            return remote(rows_of(opposite, 0), relay.at[h, 0], *sems, at_x(1))
        if kind == 1:
            return remote(rows_of(opposite, 1), relay.at[h, 1], *sems, at_x(-1))
        if kind == 2:
            return remote(rows_of(ahead_at, 1), nextto.at[h, 0, lower], *sems, at_x(1))
        if kind == 3:
            return remote(rows_of(behind_at, 0), nextto.at[h, 1, upper], *sems, at_x(-1))
        if kind == 4:
            return remote(merged.at[h, 0], nextto.at[h, 0, upper], *sems, at_x(1))
        return remote(merged.at[h, 1], nextto.at[h, 1, lower], *sems, at_x(-1))

    def y_copy(h):
        return remote(ysum.at[h], yget.at[h], ls.at[h], lr.at[h], other_y)

    owner = xx
    ahead = jnp.full((8, lanes), owner, jnp.int32) >= yc

    def lse_copy(g):
        return remote(wsend.at[g], wrecv.at[g], wss.at[g], wsr.at[g], at_plane(-g))

    def window_stage(h, stage):
        if stage == 0:
            if h == 0:
                for i, g in enumerate((1, 2)):
                    for v in range(2):
                        qcat[v, i * rows : (i + 1) * rows] = qbuf[take(behind[g], rows)]
            else:
                for v, g in enumerate((0, REACH)):
                    qcat[v, two : two + rows] = qbuf[take(behind[3], rows)]
                    qcat[v, two + rows : wide] = qbuf[take(behind[g], rows)]

            def one(y):
                at = take(y, rows)
                st[h, at] = dot(pbuf[at], qcat[version(y), h * two : (h + 1) * two], 1, 1)

            loop(0, PLANE, one)
            for kind in range(2):
                x_copy(h, kind).start()
        elif stage == 1:
            for side, start in ((0, block(1)), (1, block(-1))):
                x_copy(h, side).wait_recv()
                at = pl.ds(pl.multiple_of(start + side * chunk, 32), chunk)
                merged[h, side] = st[h, at] + relay[h, side]
                x_copy(h, 4 + side).start()
            for kind in (2, 3):
                x_copy(h, kind).start()
        elif stage == 2:
            for kind in range(2, 6):
                x_copy(h, kind).wait_recv()
            for keep, start in ((True, yy), (False, 1 - yy)):
                inner = take(start, chunk)
                at = pl.ds(pl.multiple_of(block(0) + start * chunk, 32), chunk)
                total = st[h, at] + nextto[h, 0, inner] + nextto[h, 1, inner]
                if keep:
                    mine[h] = total
                else:
                    ysum[h] = total
            y_copy(h).start()
        else:
            y_copy(h).wait_recv()
            total = (mine[h] + yget[h]) * scale
            sc[h] = total
            top = jnp.max(total, axis=0, keepdims=True)
            lse = top + jnp.log(jnp.sum(jnp.exp(total - top), axis=0, keepdims=True))
            lse = jnp.broadcast_to(lse, (8, two))
            one, another = lse[:, :lanes], pltpu.roll(lse, rows, 1)[:, :lanes]
            if h == 0:
                wsend[1] = one
                wsend[2] = another
                lse_copy(2).start()
                lse_copy(1).start()
            else:
                wsend[3] = one
                wsend[0] = jnp.where(ahead, another, LOW)
                wsend[REACH] = jnp.where(ahead, LOW, another)
                lse_copy(REACH).start()
                lse_copy(3).start()

    first = half // 2
    jobs, left = [], list(range(half))
    for s in range(1, half + 1):
        early = 0 if s < first else 2 if s == half else 1
        jobs.append([(left.pop(0), 1) for _ in range(early) if left and left[0] <= s - 2])
        jobs.append([(s - 1, 0)])
        if s == first:
            jobs[-1] += [(left.pop(0), 1)]
    jobs[-1] += [(p, 1) for p in left]
    queue = sum(jobs, [])

    def lookup(index, values):
        found = jnp.int32(values[0])
        for i, value in enumerate(values):
            found = jnp.where(index >= i, value, found)
        return found

    ends = [sum(len(some) for some in jobs[: i + 1]) for i in range(len(jobs))]

    def queued(q):
        scored(lookup(q, [p for p, _ in queue]), lookup(q, [kind for _, kind in queue]))

    stage_at = {(0, 0): 3, (0, 1): 5, (0, 2): 9, (0, 3): 12, (1, 0): 7, (1, 1): 10, (1, 2): 13}

    def ring_move(s, i):
        up_last, down_last = last_up(i), last_down(i)

        @pl.when(s <= up_last)
        def _():
            up_copy(s, i).wait_recv()

        @pl.when(s < up_last)
        def _():
            up_copy(s + 1, i).start()

        @pl.when(s <= down_last)
        def _():
            down_copy(s, i).wait_recv()

        @pl.when(s < down_last)
        def _():
            down_copy(s + 1, i).start()

    def ring_slot(slot):
        s, i = lax.div(slot, SUB) + 1, lax.rem(slot, SUB)

        @pl.when(i == 0)
        def _():
            ring_move(s, SUB)

        ring_move(s, i)

        @pl.when(slot == 0)
        def _():
            n_copy(0).wait_recv()

        @pl.when(slot == 1)
        def _():
            p_copy(1).wait_recv()
            p_copy(2).start()
            n_copy(1).start()

        @pl.when(slot == 2)
        def _():
            p_copy(0).wait_recv()
            p_copy(2).wait_recv()

        @pl.when(slot == 2 * (first - 1))
        def _():
            n_copy(1).wait_recv()
            n_copy(2).start()
            n_copy(2).wait_recv()

        for (h, stage), when in stage_at.items():
            if stage > 0:
                pl.when(slot == when)(functools.partial(window_stage, h, stage))
        low = jnp.where(slot == 0, 0, lookup(slot - 1, ends))
        loop(low, lookup(slot, ends), queued)
        for (h, stage), when in stage_at.items():
            if stage == 0:
                pl.when(slot == when)(functools.partial(window_stage, h, stage))

    loop(0, SUB * half, ring_slot)
    window_stage(1, 3)

    parts = [wsend[0]]
    for g in range(1, REACH + 1):
        lse_copy(g).wait_recv()
        parts.append(wrecv[g])

    def folded(value):
        cuts = [value[:, c : c + 128] for c in range(0, lanes, 128)]
        return jnp.concatenate(cuts, axis=0).astype(BF16)

    def unfolded(value):
        value = value.astype(F32)
        return jnp.concatenate([value[c : c + 8] for c in range(0, lanes // 16, 8)], axis=1)

    def joined(values):
        highest = functools.reduce(jnp.maximum, values)
        return highest + jnp.log(sum(jnp.exp(value - highest) for value in values))

    window_lse = joined(parts)
    hard_sum = hp[mine_slot]
    for u in range(planes - 2, -1, -1):
        hard_copy(u).wait_recv()
        hard_sum = hard_sum + hrecv[u]
    last = lax.broadcasted_iota(jnp.int32, (8, lanes), 0) == HARD
    msg[...] = jnp.where(last, window_lse, hard_sum)

    def sum_copy(p):
        return remote(msg, arecv.at[p], ags.at[p], agr.at[p], at_dim(p))

    for p in range(1, dims):
        sum_copy(p).start()
    values = [msg[...]]
    for p in range(1, dims):
        sum_copy(p).wait_recv()
        values.append(arecv[p])
    entries = jnp.where(last, joined(values), sum(values) * scale)
    highest = jnp.max(entries, axis=0, keepdims=True)
    log_total = highest + jnp.log(jnp.sum(jnp.exp(entries - highest), axis=0, keepdims=True))
    hard_weights = jnp.exp(entries - log_total)
    hwb[mine_slot] = folded(hard_weights)
    logb[0] = jnp.broadcast_to(log_total, (8, lanes))

    def log_copy(g):
        return remote(logb.at[0], logb.at[g], los.at[g], lor.at[g], at_plane(g))

    def weight_copy(u):
        device = at_plane(-span(u))
        return remote(hwb.at[mine_slot], hwb.at[u], hws.at[u], hwr.at[u], device)

    loop(0, 4, lambda u: weight_copy(u).start())
    for g in range(1, REACH + 1):
        log_copy(g).start()
    loop(4, planes - 1, lambda u: weight_copy(u).start())

    logs = [logb[0]]
    for g in range(1, REACH + 1):
        log_copy(g).wait_recv()
        logs.append(logb[g])
    halves = [beside(logs[1:3]), beside([logs[3], jnp.where(ahead, logs[0], logs[REACH])])]
    row_at = lax.broadcasted_iota(jnp.int32, (chunk, two), 0) + yy * chunk + rows
    lane_at = lax.broadcasted_iota(jnp.int32, (chunk, two), 1)
    positive = (row_at == lane_at) & (jnp.full((chunk, two), owner, jnp.int32) == yc)
    my_tile = take(xx * DIM_Y + yy, chunk)
    wt[my_tile, 0:two] = jnp.exp(sc[0] - halves[0][0:1]).astype(BF16)
    weights = jnp.exp(sc[1] - halves[1][0:1]) - jnp.where(positive, 1.0, 0.0)
    wt[my_tile, two:wide] = weights.astype(BF16)

    def tile_copy(p):
        return remote(wt.at[my_tile], wt.at[my_tile], wts.at[p], wtr.at[p], at_dim(p))

    for p in range(1, dims):
        tile_copy(p).start()

    def graded(g):
        for i in range(PLANE):
            u = PLANE * g + i

            @pl.when(u != mine_slot)
            def _():
                weight_copy(u).wait_recv()

        ids = jnp.concatenate([idxp[2 * g], idxp[2 * g + 1]], axis=1)
        pay = beside([unfolded(hwb[PLANE * g + i]) for i in range(PLANE)])
        counted = lax.broadcasted_iota(jnp.int32, (8, wide), 0) < HARD
        high = ids >> 4
        high = jnp.where((high >= 0) & (high < PLANE * pool // 16), high, -1)
        low = ids & 15
        deep = lax.broadcasted_iota(jnp.int32, (16, wide), 0)
        keys, held = [], []
        for k in range(HARD):
            same = jnp.where((ids == ids[k : k + 1]) & counted, pay, 0.0)
            same = jnp.sum(same, axis=0, keepdims=True)
            held.append(jnp.broadcast_to(same, (16, wide)).astype(BF16))
            key = jnp.where(low[k : k + 1] == deep, high[k : k + 1], -1)
            keys.append(key.astype(F32).astype(BF16))

        for k in range(HARD):
            keyb[k] = keys[k]
            heldb[k] = held[k]

    def built(g):
        def cut_at(c):
            cut = pl.ds(pl.multiple_of(c * 128, 128), 128)
            out = pl.ds(pl.multiple_of(g * wide + c * 128, 128), 128)
            key_cut = [keyb[k, :, cut] for k in range(HARD)]
            held_cut = [heldb[k, :, cut] for k in range(HARD)]

            def one(r):
                base = jnp.full((16, 128), 8 * r, jnp.int32).astype(F32).astype(BF16)
                moved = [key - base for key in key_cut]
                for i in range(8):
                    tile = jnp.zeros((16, 128), BF16)
                    for k in range(HARD):
                        tile = jnp.where(moved[k] == jnp.bfloat16(i), held_cut[k], tile)
                    wht[pl.ds(pl.multiple_of(128 * r + 16 * i, 16), 16), out] = tile

            loop(0, PLANE * pool // 128, one)

        loop(0, wide // 128, cut_at)

    def grown(y):
        at = take(y, pool)
        dnb[at] = dot(wht[at], qbuf[...], 1, 0)

    def returned(g):
        at = pl.ds(pl.multiple_of(g * wide, 128), wide)
        cbuf[take(g, wide)] += dot(wht[:, at], nbuf[...], 0, 0)

    def window_documents():
        def one(y):
            at = take(y, rows)
            dpb[at] = dot(wt[at], qcat[version(y)], 1, 0)

        loop(0, PLANE, one)

    tail = wide - lanes

    def window_queries():
        for p in range(1, dims):
            tile_copy(p).wait_recv()
        win[0:tail] = dot(wt[:, 0:tail], pbuf[...], 0, 0)
        for g in range(1, REACH - 1):
            cbuf[take(behind[g], rows)] += win[(g - 1) * rows : g * rows]

    def window_ends():
        near = jnp.zeros((lanes, feats), F32)
        rest = jnp.zeros((lanes, feats), F32)
        for y in range(PLANE):
            at = pl.ds(y * rows, rows)
            piece = dot(wt[at, tail:wide], pbuf[at], 0, 0)
            here = jnp.full((lanes, feats), y, jnp.int32) >= yc
            near = near + jnp.where(here, piece, 0.0)
            rest = rest + jnp.where(here, 0.0, piece)
        win[tail:wide] = near + rest
        cbuf[take(behind[3], rows)] += win[two:two + rows]
        cbuf[take(mine_slot, rows)] += near[lanes - rows : lanes]
        cbuf[take(behind[REACH], rows)] += rest[lanes - rows : lanes]

    def a_copy(t, i):
        at = pl.ds(pl.multiple_of(i * part, 16), part)
        sems = (as_.at[t + 1, i], ar.at[t + 1, i])
        return remote(senda.at[t, at], recva.at[t + 1, at], *sems, down)

    def b_copy(t, i):
        at = pl.ds(pl.multiple_of(i * part, 16), part)
        sems = (bs.at[t + 1, i], br.at[t + 1, i])
        return remote(sendb.at[t, at], recvb.at[t + 1, at], *sems, up)

    def core_copy(kind):
        src, dst = ((nsend, nrecv), (psend, precv))[kind]
        return remote(src, dst, cs.at[kind], cr.at[kind], core)

    def far_copy(kind):
        src, dst = ((nfar, ngot), (pfar, pgot))[kind]
        return remote(src, dst, ys.at[kind], yr.at[kind], far)

    def core_stage(kind):
        total, size, send = ((dnb, pool, nsend), (dpb, rows, psend))[kind]
        for i, y in enumerate((core_yc, cross_yc)):
            send[i] = total[take(y, size)].astype(BF16)
        core_copy(kind).start()

    def far_stage(kind):
        total, size, got, send = ((dnb, pool, nrecv, nfar), (dpb, rows, precv, pfar))[kind]
        core_copy(kind).wait_recv()
        send[...] = (total[take(far_yc, size)] + got[1].astype(F32)).astype(BF16)
        far_copy(kind).start()

    def back_slot(slot):
        @pl.when(slot >= 1)
        def _():
            t, i = lax.div(slot - 1, SUB), lax.rem(slot - 1, SUB)
            for begin, u, copy, got, send in (
                (first_a(i), jnp.maximum(2 * t - 1, 0), a_copy, recva, senda),
                (first_b(i), 2 * t, b_copy, recvb, sendb),
            ):

                @pl.when(t > begin)
                def _():
                    copy(t - 1, i).wait_recv()

                @pl.when(t >= begin)
                def _():
                    at = pl.ds(pl.multiple_of(i * part, 16), part)
                    piece = cbuf[pl.ds(pl.multiple_of(u * rows + i * part, 16), part)]
                    send[t, at] = (piece + got[t, at].astype(F32)).astype(BF16)
                    copy(t, i).start()

        @pl.when(slot < groups)
        def _():
            graded(slot)
            built(slot)

        @pl.when((slot == 0) | (slot == 4) | (slot == 7) | (slot == 10))
        def _():
            returned(lax.div(slot, 3))

        @pl.when((slot == 5) | (slot == 6))
        def _():
            grown(jnp.where(slot == 5, core_yc, far_yc))
            grown(jnp.where(slot == 5, cross_yc, yc))

        pl.when(slot == 5)(functools.partial(core_stage, 0))
        pl.when(slot == 7)(functools.partial(far_stage, 0))

        @pl.when(slot == 8)
        def _():
            window_queries()
            window_ends()

        @pl.when(slot == 9)
        def _():
            window_documents()
            core_stage(1)

        pl.when(slot == 11)(functools.partial(far_stage, 1))

    loop(0, SUB * half + 1, back_slot)

    for kind, total, size, got, crossed, out in (
        (0, dnb, pool, nrecv, ngot, dn_out),
        (1, dpb, rows, precv, pgot, dp_out),
    ):
        far_copy(kind).wait_recv()
        back = got[0].astype(F32) + crossed[...].astype(F32)
        out[...] = total[take(yc, size)] + back
    for i in range(SUB):
        a_copy(half - 1, i).wait_recv()
        b_copy(half - 1, i).wait_recv()
    back = recva[half].astype(F32) + recvb[half].astype(F32)
    gq_out[...] = cbuf[take(mine_slot, rows)] + back

    for i in range(SUB + 1):
        loop(1, last_up(i) + 1, lambda s: up_copy(s, i).wait_send())
        loop(1, last_down(i) + 1, lambda s: down_copy(s, i).wait_send())
    for i in range(3):
        p_copy(i).wait_send()
        n_copy(i).wait_send()
    for h in range(2):
        for kind in range(6):
            x_copy(h, kind).wait_send()
        y_copy(h).wait_send()
    for p in range(1, dims):
        sum_copy(p).wait_send()
        tile_copy(p).wait_send()
    for g in range(1, REACH + 1):
        lse_copy(g).wait_send()
        log_copy(g).wait_send()
    loop(0, planes - 1, lambda u: hard_copy(u).wait_send())
    loop(0, planes - 1, lambda u: weight_copy(u).wait_send())
    for i in range(SUB):
        loop(first_a(i), half, functools.partial(lambda i, t: a_copy(t, i).wait_send(), i))
        loop(first_b(i), half, lambda t: b_copy(t, i).wait_send())
    for kind in range(2):
        core_copy(kind).wait_send()
        far_copy(kind).wait_send()


def on_device(queries, passages, negatives, hard_index):
    rows, feats = queries.shape
    pool = negatives.shape[0]
    planes = lax.axis_size("blk") // PLANE
    dims = lax.axis_size("dim")
    half = planes // 2
    wide, two = PLANE * rows, 2 * rows
    chunk = wide // dims
    lanes = -(-rows // 128) * 128

    dma = pltpu.SemaphoreType.DMA
    vmem = pltpu.VMEM
    scratch = [
        vmem((planes * rows, feats), BF16),
        vmem((HARD, rows), jnp.int32),
        vmem((planes, 8, lanes), jnp.int32),
        vmem((half, 8, two), jnp.int32),
        vmem((wide, feats), BF16),
        vmem((PLANE * pool, feats), BF16),
        vmem((2, wide, feats), BF16),
        vmem((2, wide, two), F32),
        vmem((2, 2, chunk, two), F32),
        vmem((2, 2, chunk, two), F32),
        vmem((2, 2, 2 * chunk, two), F32),
        vmem((2, chunk, two), F32),
        vmem((2, chunk, two), F32),
        vmem((2, chunk, two), F32),
        vmem((2, chunk, two), F32),
        vmem((half, 8, two), F32),
        vmem((planes, 8, lanes), F32),
        vmem((planes, 8, lanes), F32),
        vmem((REACH + 1, 8, lanes), F32),
        vmem((REACH + 1, 8, lanes), F32),
        vmem((8, lanes), F32),
        vmem((dims, 8, lanes), F32),
        vmem((planes, lanes // 16, 128), BF16),
        vmem((REACH + 1, 8, lanes), F32),
        vmem((wide, wide), BF16),
        vmem((HARD, 16, wide), BF16),
        vmem((HARD, 16, wide), BF16),
        vmem((PLANE * pool, planes * rows), BF16),
        vmem((planes * rows, feats), F32),
        vmem((wide, feats), F32),
        vmem((PLANE * pool, feats), F32),
        vmem((wide, feats), F32),
        vmem((half + 1, rows, feats), BF16),
        vmem((half + 1, rows, feats), BF16),
        vmem((half, rows, feats), BF16),
        vmem((half, rows, feats), BF16),
        vmem((2, pool, feats), BF16),
        vmem((2, pool, feats), BF16),
        vmem((2, rows, feats), BF16),
        vmem((2, rows, feats), BF16),
        vmem((pool, feats), BF16),
        vmem((pool, feats), BF16),
        vmem((rows, feats), BF16),
        vmem((rows, feats), BF16),
        dma((4,)),
    ]
    for shape in (
        (half + 1, SUB + 1), (half + 1, SUB + 1), (3,), (3,), (2, 6), (2,), (planes,), (REACH + 1,),
        (dims,), (planes,), (REACH + 1,), (dims,), (half + 1, SUB), (half + 1, SUB), (2,), (2,),
    ):
        scratch += [dma(shape), dma(shape)]

    sums = pl.pallas_call(
        functools.partial(kernel, planes, dims),
        out_shape=(
            jax.ShapeDtypeStruct((rows, feats), F32),
            jax.ShapeDtypeStruct((rows, feats), F32),
            jax.ShapeDtypeStruct((pool, feats), F32),
        ),
        in_specs=[pl.BlockSpec(memory_space=pltpu.HBM)] * 4,
        out_specs=[pl.BlockSpec(memory_space=pltpu.VMEM)] * 3,
        scratch_shapes=scratch,
        compiler_params=pltpu.CompilerParams(
            collective_id=0, has_side_effects=True, vmem_limit_bytes=60 * 1024 * 1024
        ),
    )(queries, passages, negatives, hard_index.T)
    return tuple(total * scale for total in sums)


def solution(mesh):
    placed = (P("blk", "dim"), P("blk", "dim"), P("blk", "dim"), P("blk", None))
    return jax.shard_map(
        on_device,
        mesh=mesh,
        in_specs=placed,
        out_specs=(P("blk", "dim"), P("blk", "dim"), P("blk", "dim")),
        check_vma=False,
    )
```
